512 devices in a mesh: lat: 8 (over x_lo, y), lon: 64 (over x_hi, z, core).
Axes of the slice: x: 4 (x_hi: 2, x_lo: 2; x = x_hi * 2 + x_lo), y: 4, z: 16, core: 2. Of those that a mesh axis runs over, the one named last changes fastest.
Arguments:
- signal: bfloat16 [384, 512, 256], P('lat', 'lon'), may hold values from -6 to 6
- cotangent: bfloat16 [384, 512, 256], P('lat', 'lon'), may hold values from -6 to 6
- weights: bfloat16 [4, 256, 256], replicated, may hold values from -0.1875 to 0.1875
- band_kernel: bfloat16 [4, 384, 3, 17], replicated, may hold values from -1.25 to 1.25
- cycle_kernel: bfloat16 [4, 4, 3, 512], replicated, may hold values from -0.15625 to 0.15625
- support_width: int32 [384], replicated, may hold values from 1 to 8, as said below
Outputs:
- conv_output: bfloat16 [384, 512, 256], P('lat', 'lon')
- signal_grad: bfloat16 [384, 512, 256], P('lat', 'lon')
- weight_grad: float32 [4, 256, 256], replicated
The draws below stay inside these ranges and needn't reach their ends.
Inputs may be any that keep to these rules, and one draw needn't show every extreme that they name: `support_width`: some row has the half-width 8.
All inputs are finite; a program needn't handle non-finite values.
Results may differ from the reference program's by a relative error of at most 0.0049.
Values may be sent and summed in bfloat16 or wider, within the bound.
A program may use at most 64 MiB of HBM per device.

```python
import jax
import jax.numpy as jnp
from jax import lax

C = 256
K = 4
R = 1
H = 8
P_SIZE = 2
NLAT = 384
NLON = 512


def draw_support_width(key, part):
    key = jax.random.fold_in(key, 7)
    first_key, second_key = jax.random.split(key)
    widths = jax.random.randint(first_key, (NLAT,), 1, H + 1, dtype=jnp.int32)
    chosen = jax.random.randint(second_key, (), 0, NLAT, dtype=jnp.int32)
    return jnp.where(jnp.arange(NLAT, dtype=jnp.int32) == chosen, H, widths).astype(jnp.int32)


def shard_levels(own_key, shape, cuts, least, largest):
    level, own = 1.0, jax.random.fold_in(own_key, 6)
    for dim, blocks in cuts:
        steps = jnp.exp(jax.random.uniform(jax.random.fold_in(own, dim), (blocks,), jnp.float32, least / len(cuts), largest / len(cuts)))
        level = level * jnp.repeat(steps, shape[dim] // blocks).reshape([-1 if axis == dim else 1 for axis in range(len(shape))])
    return level


def normal_values(own_key, dims, width, most, cuts=(), held_as=jnp.bfloat16):
    drawn = jax.random.normal(own_key, dims, jnp.float32) * width
    if len(cuts) > 0:
        drawn = shard_levels(own_key, dims, cuts, -0.22, 0.18) * drawn
    return jnp.clip(drawn, min=-most, max=most).astype(held_as)


def setup_inputs(seed: int = 0) -> dict:
    seeds = jax.random.split(jax.random.key(seed), 7)
    return {
        "signal": normal_values(seeds[0], (NLAT, NLON, C), 1.0, 6.0, ((0, 8), (1, 64))),
        "cotangent": normal_values(seeds[1], (NLAT, NLON, C), 1.0, 6.0, ((0, 8), (1, 64))),
        "weights": normal_values(seeds[2], (K, C, C), (K * C) ** -0.5, 0.1875),
        "band_kernel": normal_values(seeds[3], (K, NLAT, 2 * R + 1, 2 * H + 1), ((2 * R + 1) * (H + 1)) ** -0.5, 1.25),
        "cycle_kernel": normal_values(seeds[4], (K, 2 * P_SIZE, 2 * R + 1, NLON), ((2 * R + 1) * NLON) ** -0.5, 0.15625),
        "support_width": draw_support_width(jax.random.fold_in(seeds[6], 71), 0),
    }


precise = lax.Precision.HIGHEST

def band_coefficients(band_kernel, support_width):
    offsets = jnp.abs(jnp.arange(2 * H + 1, dtype=jnp.int32) - H)
    row_ids = jnp.arange(NLAT, dtype=jnp.int32)
    polar_rows = (row_ids < P_SIZE) | (row_ids >= NLAT - P_SIZE)
    allowed = (offsets[None, :] <= support_width[:, None]) & jnp.logical_not(polar_rows)[:, None]
    return band_kernel.astype(jnp.float32) * allowed[None, :, None, :].astype(jnp.float32)

def reference(signal, cotangent, weights, band_kernel, cycle_kernel, support_width):
    coeffs = band_coefficients(band_kernel, support_width)
    coeff_pad = jnp.pad(coeffs, ((0, 0), (R, R), (0, 0), (0, 0)))
    signal_pad = jnp.pad(signal, ((R, R), (0, 0), (0, 0)))
    cot_pad = jnp.pad(cotangent, ((R, R), (0, 0), (0, 0)))
    weights_full = weights.astype(jnp.float32)
    cycle_full = cycle_kernel.astype(jnp.float32)
    lon_ids = jnp.arange(NLON, dtype=jnp.int32)
    circ_index = (lon_ids[:, None] - lon_ids[None, :]) % NLON
    trans_index = (lon_ids[None, :] - lon_ids[:, None]) % NLON

    def band_row(row_index):
        window = lax.dynamic_slice_in_dim(signal_pad, row_index, 2 * R + 1, 0).astype(jnp.float32)
        shifted = jnp.stack([jnp.roll(window, shift_index - H, axis=1) for shift_index in range(2 * H + 1)], axis=1)
        coeff_row = lax.dynamic_index_in_dim(coeffs, row_index, 1, keepdims=False)
        return jnp.einsum('krd,rdlc->klc', coeff_row, shifted, precision=precise)

    def polar_row(row_index):
        pole_row = jnp.where(row_index < P_SIZE, row_index, row_index - NLAT + 2 * P_SIZE)
        window = lax.dynamic_slice_in_dim(signal_pad, row_index, 2 * R + 1, 0).astype(jnp.float32)
        kernel_row = lax.dynamic_index_in_dim(cycle_full, pole_row, 1, keepdims=False)
        circulant = kernel_row[:, :, circ_index]
        return jnp.einsum('krlm,rmc->klc', circulant, window, precision=precise)

    def forward_step(weight_sum, row_index):
        is_polar = (row_index < P_SIZE) | (row_index >= NLAT - P_SIZE)
        filtered = lax.cond(is_polar, polar_row, band_row, row_index)
        filtered = lax.optimization_barrier(filtered.astype(jnp.bfloat16))
        filtered_full = filtered.astype(jnp.float32)
        out_row = jnp.einsum('klc,kce->le', filtered_full, weights_full, precision=precise).astype(jnp.bfloat16)
        cot_row = lax.dynamic_index_in_dim(cotangent, row_index, 0, keepdims=False).astype(jnp.float32)
        weight_sum = weight_sum + jnp.einsum('klc,le->kce', filtered_full, cot_row, precision=precise)
        return (weight_sum, out_row)
    all_rows = jnp.arange(NLAT, dtype=jnp.int32)
    weight_sum, conv_output = lax.scan(forward_step, jnp.zeros((K, C, C), jnp.float32), all_rows)
    weight_grad = weight_sum / jnp.sqrt(jnp.float32(NLAT * NLON))

    def mixed_of(cot_rows):
        mixed = jnp.einsum('ile,kce->kilc', cot_rows.astype(jnp.float32), weights_full, precision=precise)
        return lax.optimization_barrier(mixed.astype(jnp.bfloat16))
    cot_polar = jnp.concatenate([cotangent[:P_SIZE], cotangent[NLAT - P_SIZE:]], axis=0)
    mixed_polar = mixed_of(cot_polar).astype(jnp.float32)

    def pole_terms(pole):
        terms = jnp.zeros((P_SIZE + 2 * R, NLON, C), jnp.float32)
        for offset in range(P_SIZE):
            for lat_tap in range(2 * R + 1):
                kernel_row = cycle_full[:, pole * P_SIZE + offset, lat_tap]
                matrix = kernel_row[:, trans_index]
                contrib = jnp.einsum('kml,klc->mc', matrix, mixed_polar[:, pole * P_SIZE + offset], precision=precise)
                terms = terms.at[offset + lat_tap].add(contrib)
        return terms
    polar_extra = jnp.concatenate([pole_terms(0)[R:], pole_terms(1)[:P_SIZE + R]], axis=0)

    def backward_step(carry_window, row_index):
        fresh = lax.dynamic_slice_in_dim(cot_pad, row_index + 2 * R, 1, 0)
        full_window = jnp.concatenate([carry_window, mixed_of(fresh)], axis=1)
        coeff_rows = lax.dynamic_slice_in_dim(coeff_pad, row_index, 2 * R + 1, 1)
        coeff_sel = jnp.stack([coeff_rows[:, 2 * R - lat_tap, lat_tap] for lat_tap in range(2 * R + 1)], axis=1)
        reversed_rows = full_window[:, ::-1].astype(jnp.float32)
        shifted = jnp.stack([jnp.roll(reversed_rows, H - shift_index, axis=2) for shift_index in range(2 * H + 1)], axis=2)
        total = jnp.einsum('krd,krdlc->lc', coeff_sel, shifted, precision=precise)
        is_top = row_index < P_SIZE + R
        is_bottom = row_index >= NLAT - P_SIZE - R
        picked = jnp.where(is_top, row_index, row_index - (NLAT - P_SIZE - R) + (P_SIZE + R))
        picked = jnp.clip(picked, 0, 2 * (P_SIZE + R) - 1).astype(jnp.int32)
        extra_row = lax.dynamic_index_in_dim(polar_extra, picked, 0, keepdims=False)
        total = total + jnp.where(is_top | is_bottom, extra_row, jnp.zeros_like(extra_row))
        return (full_window[:, 1:], total.astype(jnp.bfloat16))
    first_window = mixed_of(cot_pad[:2 * R])
    last_window, signal_grad = lax.scan(backward_step, first_window, all_rows)
    return (conv_output, signal_grad, weight_grad)
```

```python
import functools
import math

import jax
import jax.numpy as jnp
from jax import lax
from jax.experimental import pallas as pl
from jax.experimental.pallas import tpu as pltpu
from jax.sharding import PartitionSpec as P

K = 4
R = 1
H = 8
P_SIZE = 2
L = 8
SLAB = P_SIZE + R
X_HI = 2
X_LO = 2
XS = X_HI * X_LO
MESH = pl.DeviceIdType.MESH
F32 = jnp.float32
BF16 = jnp.bfloat16


def dot(a, b):
    return jnp.dot(a, b, preferred_element_type=F32)


def kernel(
    sig, cot, w_hbm, bf_hbm, bb_hbm, rev_hbm, cyc_hbm,
    conv_out, sgrad_out, wgrad_out,
    s_o, s_l, s_r, c_o, c_l, c_r, w, bf, bb, rev, cyc,
    amat, bmat, filt, grad, cot2, conv_v, sg_v,
    slab, qf, qb,
    wown, wsend, wrecv, half, xs, xr, zs, zr, za, fin, wg_v,
    load_sem, halo_ss, halo_rs, px_sem, rr_ss, rr_rs, rl_ss, rl_rs, pf_ss, pf_rs,
    core_sem, x_ss, x_rs, z_ss, z_rs, za_ss, za_rs, xa_ss, xa_rs, fc_sem, out_sem,
):
    rows, _, chans = sig.shape
    nlat, nlon = lax.axis_size("lat"), lax.axis_size("lon")
    ys, zn = nlat // X_LO, nlon // (2 * X_HI)
    lat, lon = lax.axis_index("lat"), lax.axis_index("lon")
    x_lo, y = lat // ys, lat % ys
    x_hi, z, core = lon // (2 * zn), (lon // 2) % zn, lon % 2
    x = x_hi * X_LO + x_lo
    me_q = x * ys + y
    nq = XS * ys
    blocks = rows // 8
    is_top = lat == 0
    is_polar = is_top | (lat == nlat - 1)

    def place(xx, yy, zz, cc):
        return {"lat": (xx % X_LO) * ys + yy, "lon": (xx // X_LO) * (2 * zn) + zz * 2 + cc}

    def xy_peer(o):
        xx, yy = (x + o // ys) % XS, (y + o % ys) % ys
        return xx * ys + yy, place(xx, yy, z, core)

    def z_peer(d):
        zz = (z + d) % zn
        return zz, place(x, y, zz, core)

    def beside(dlat, dlon):
        return {"lat": (lat + dlat + nlat) % nlat, "lon": (lon + dlon + nlon) % nlon}

    partner = place(x, y, z, 1 - core)

    def remote(src, dst, ss, rs, dev):
        return pltpu.make_async_remote_copy(
            src_ref=src, dst_ref=dst, send_sem=ss, recv_sem=rs, device_id=dev, device_id_type=MESH
        )

    loads = [
        pltpu.make_async_copy(a, b, load_sem.at[i])
        for i, (a, b) in enumerate((
            (bf_hbm, bf), (sig, s_o.at[pl.ds(1, rows)]), (cot, c_o.at[pl.ds(1, rows)]),
            (bb_hbm, bb), (rev_hbm, rev), (cyc_hbm, cyc), (w_hbm, w),
        ))
    ]
    for copy in loads:
        copy.start()

    barrier = pltpu.get_barrier_semaphore()

    def greet(dev):
        pl.semaphore_signal(barrier, inc=1, device_id=dev, device_id_type=MESH)

    for dlat, dlon in ((0, 1), (0, -1), (1, 1), (1, -1), (-1, 1), (-1, -1)):
        greet(beside(dlat, dlon))

    def greet_xy(o, c):
        greet(xy_peer(o)[1])
        return c

    def greet_z(d, c):
        greet(z_peer(d)[1])
        return c

    lax.fori_loop(1, nq, greet_xy, 0)
    lax.fori_loop(1, zn, greet_z, 0)
    pl.semaphore_wait(barrier, 6 + (nq - 1) + (zn - 1))

    def halo_copies(src, own, left, right, n):
        last, first = src.at[pl.ds(rows - 1, 1)], src.at[pl.ds(0, 1)]
        top, bottom = pl.ds(0, 1), pl.ds(rows + 1, 1)
        spec = (
            (src, left.at[pl.ds(1, rows)], beside(0, 1)),
            (src, right.at[pl.ds(1, rows)], beside(0, -1)),
            (last, own.at[top], beside(1, 0)),
            (last, left.at[top], beside(1, 1)),
            (last, right.at[top], beside(1, -1)),
            (first, own.at[bottom], beside(-1, 0)),
            (first, left.at[bottom], beside(-1, 1)),
            (first, right.at[bottom], beside(-1, -1)),
        )
        return [
            remote(a, b, halo_ss.at[n + i], halo_rs.at[n + i], dev)
            for i, (a, b, dev) in enumerate(spec)
        ]

    slab_at = jnp.where(is_top, 0, rows - SLAB)
    pole_at = jnp.where(is_top, 0, rows - P_SIZE)
    slab_src = (sig.at[pl.ds(slab_at, SLAB)], cot.at[pl.ds(pole_at, P_SIZE)])
    mine = (slab.at[pl.ds(0, SLAB), x_hi, z, core], slab.at[pl.ds(SLAB, P_SIZE), x_hi, z, core])
    x_other = place((x + X_LO) % XS, y, z, core)

    @pl.when(is_polar)
    def _():
        for i in range(2):
            pltpu.make_async_copy(slab_src[i], mine[i], px_sem.at[i]).start()
            remote(slab_src[i], mine[i], px_sem.at[2 + i], px_sem.at[4 + i], x_other).start()

    sig_halo = halo_copies(sig, s_o, s_l, s_r, 0)
    cot_halo = halo_copies(cot, c_o, c_l, c_r, 8)
    for copy in sig_halo + cot_halo:
        copy.start()

    def build(src, dst):
        def block(b, c):
            for k in range(K):
                tile = src[k, pl.ds(pl.multiple_of(b * 8, 8), 8), :]
                for i in range(0, 8, 2):
                    parts = [
                        pltpu.roll(
                            jnp.broadcast_to(tile[j : j + 1], (L, tile.shape[1])),
                            j * 3 * L, 1, stride=1, stride_axis=0,
                        )
                        for j in (i, i + 1)
                    ]
                    dst[b, pl.ds((k * 8 + i) * L, 2 * L), :] = jnp.concatenate(parts, 0).astype(BF16)
            return c

        lax.fori_loop(0, blocks, block, 0)

    def window(o, left, right, b):
        at = pl.ds(b * 8, 10)
        parts = [ref[at].astype(F32) for ref in (left, o, right)]
        both = jnp.concatenate(parts, 1).reshape(30 * L, chans)
        return jnp.concatenate([both, jnp.zeros((2 * L, chans), F32)], 0).astype(BF16)

    def cycle_rows(src, r):
        row = jnp.broadcast_to(src[r : r + 1, :], (L, src.shape[1]))
        return pltpu.roll(row, 0, 1, stride=1, stride_axis=0)

    loads[0].wait()
    build(bf, amat)
    loads[3].wait()
    build(bb, bmat)

    circle = nlon * L
    loads[4].wait()
    loads[5].wait()

    @pl.when(is_polar)
    def _():
        rev[...] = pltpu.roll(rev[...], lon * L, 1)
        cyc[...] = pltpu.roll(cyc[...], lon * L, 1)
        for k in range(K):
            for r in range(SLAB):
                at = (k * SLAB + r) * P_SIZE
                rows_f = [cycle_rows(rev, at + p) for p in range(P_SIZE)]
                qf[pl.ds(k * 16, 16), pl.ds(r * circle, circle)] = jnp.concatenate(rows_f, 0).astype(BF16)
        for kj in range(0, K * SLAB, 2):
            for p in range(P_SIZE):
                rows_b = [cycle_rows(cyc, (kj + t) * P_SIZE + p) for t in range(2)]
                qb[pl.ds(kj * L, 16), pl.ds(p * circle, circle)] = jnp.concatenate(rows_b, 0).astype(BF16)

    hops = zn // 2

    def block_at(b):
        return slab.at[:, :, b, core]

    def ring_right(t):
        blk = block_at((z - t + zn) % zn)
        return remote(blk, blk, rr_ss.at[t], rr_rs.at[t], z_peer(1)[1])

    def ring_left(t):
        blk = block_at((z + t) % zn)
        return remote(blk, blk, rl_ss.at[t], rl_rs.at[t], z_peer(zn - 1)[1])

    def pass_on(b, n):
        blk = block_at(b)
        return remote(blk, blk, pf_ss.at[n], pf_rs.at[n], partner)

    @pl.when(is_polar)
    def _():
        for i in range(2):
            pltpu.make_async_copy(slab_src[i], mine[i], px_sem.at[i]).wait()
        for i in range(2):
            remote(slab_src[i], mine[i], px_sem.at[2 + i], px_sem.at[4 + i], x_other).wait()

        def step(t, c):
            ring_right(t).start()

            @pl.when(t < hops - 1)
            def _():
                ring_left(t).start()

            pass_on((z - t + zn) % zn, t).start()

            @pl.when((t > 0) & (t < hops))
            def _():
                pass_on((z + t) % zn, hops + t).start()

            ring_right(t).wait_recv()

            @pl.when(t < hops - 1)
            def _():
                ring_left(t).wait_recv()

            return c

        lax.fori_loop(0, hops, step, 0)
        pass_on((z - hops + zn) % zn, hops).start()

    loads[1].wait()
    for copy in sig_halo:
        copy.wait_recv()

    def forward(b, c):
        part = dot(amat[b], window(s_o, s_l, s_r, b)).astype(BF16)
        for k in range(K):
            filt[k, pl.ds(b * 64, 64), :] = part[k * 64 : (k + 1) * 64]
        return c

    lax.fori_loop(0, blocks, forward, 0)
    loads[2].wait()

    def fold(b, c):
        cot2[pl.ds(b * 64, 64), :] = (
            c_o[pl.ds(1 + b * 8, 8)].astype(F32).reshape(64, chans).astype(BF16)
        )
        return c

    lax.fori_loop(0, blocks, fold, 0)

    def circle_of(r):
        return slab[r].astype(F32).reshape(circle, chans).astype(BF16)

    @pl.when(is_polar)
    def _():
        def step(t, c):
            pass_on((z - t + zn) % zn, t).wait()
            return c

        lax.fori_loop(0, zn, step, 0)

        def sent(t, c):
            ring_right(t).wait_send()

            @pl.when(t < hops - 1)
            def _():
                ring_left(t).wait_send()

            return c

        lax.fori_loop(0, hops, sent, 0)
        part = sum(dot(qf[:, r * circle : (r + 1) * circle], circle_of(r)) for r in range(SLAB))
        at = pl.multiple_of(jnp.where(is_top, 0, (rows - P_SIZE) * L), 16)
        for k in range(K):
            filt[k, pl.ds(at, 16), :] = part[k * 16 : (k + 1) * 16].astype(BF16)

    def weight_part(k):
        return lax.dot_general(
            filt[k], cot2[...], (((0,), (0,)), ((), ())), preferred_element_type=F32
        )

    per_core = K // 2
    for i in range(per_core):
        wsend[pl.ds(i * chans, chans), :] = weight_part((1 - core) * per_core + i).astype(BF16)
    to_core = remote(wsend, wrecv, core_sem.at[0], core_sem.at[1], partner)
    to_core.start()
    for i in range(per_core):
        wown[pl.ds(i * chans, chans), :] = weight_part(core * per_core + i)

    piece = per_core * chans // nq
    to_core.wait_recv()
    summed = wown[...] + wrecv[...].astype(F32)
    half[...] = summed.reshape(nq, piece, chans)
    xs[...] = summed.astype(BF16).reshape(nq, piece, chans)

    def xy_copy(o):
        q, dev = xy_peer(o)
        return remote(xs.at[q], xr.at[o], x_ss.at[o], x_rs.at[o], dev)

    def loop(lo, hi, f):
        def body(i, c):
            f(i)
            return c

        lax.fori_loop(lo, hi, body, 0)

    loop(1, nq, lambda o: xy_copy(o).start())

    loads[6].wait()
    chunk = 8

    def mix_out(b):
        at = pl.ds(b * chunk * L, chunk * L)
        acc = sum(dot(filt[k, at, :], w[k]) for k in range(K))
        conv_v[pl.ds(b * chunk, chunk)] = acc.reshape(chunk, L, chans).astype(BF16)

    loop(0, rows // chunk, mix_out)
    conv_copy = pltpu.make_async_copy(conv_v, conv_out, out_sem.at[0])
    conv_copy.start()

    loop(1, nq, lambda o: xy_copy(o).wait_recv())
    total = half[me_q]
    for o in range(1, nq):
        total = total + xr[o].astype(F32)
    owners = zn // 2
    tiles = piece * chans // (owners * 8 * 128)
    for t in range(owners * tiles):
        r, h = t // (chans // 128), t % (chans // 128)
        zs[t // tiles, t % tiles] = total[r * 8 : (r + 1) * 8, h * 128 : (h + 1) * 128]

    def z_copy(d):
        zz, dev = z_peer(d)
        return remote(zs.at[zz % owners], zr.at[d], z_ss.at[d], z_rs.at[d], dev)

    loop(1, zn, lambda d: z_copy(d).start())

    for copy in cot_halo:
        copy.wait_recv()

    def backward(b):
        part = dot(bmat[b], window(c_o, c_l, c_r, b))
        for k in range(K):
            grad[k, pl.ds(b * 64, 64), :] = part[k * 64 : (k + 1) * 64]

    loop(0, blocks, backward)

    loop(1, zn, lambda d: z_copy(d).wait_recv())
    zr[0] = zs[z % owners]
    acc = zr[0] + zr[owners]
    for d in range(1, owners):
        acc = acc + (zr[d] + zr[d + owners])
    za[z % owners] = acc * F32(1.0 / math.sqrt(rows * nlat * L * nlon))

    def za_copy(i):
        d = i + 1 + jnp.where(i >= owners // 2, zn - owners, 0)
        dst = za.at[z % owners]
        return remote(dst, dst, za_ss.at[i], za_rs.at[i], z_peer(d)[1])

    loop(0, owners - 1, lambda i: za_copy(i).start())

    @pl.when(is_polar)
    def _():
        extra = sum(
            dot(qb[:, p * circle : (p + 1) * circle], circle_of(SLAB + p)) for p in range(P_SIZE)
        )
        at = pl.multiple_of(jnp.where(is_top, 0, (rows - SLAB) * L), 8)
        for k in range(K):
            grad[k, pl.ds(at, SLAB * L), :] += extra[k * SLAB * L : (k + 1) * SLAB * L]

    loop(0, owners - 1, lambda i: za_copy(i).wait_recv())
    lanes = chans // 128
    lines = []
    for r in range(piece // 8):
        line = [
            za[(r * lanes + h) // tiles, (r * lanes + h) % tiles] for h in range(lanes)
        ]
        lines.append(jnp.concatenate(line, 1))
    fin[core, me_q] = jnp.concatenate(lines, 0).astype(BF16)

    def xa_copy(o):
        dst = fin.at[core, me_q]
        return remote(dst, dst, xa_ss.at[o], xa_rs.at[o], xy_peer(o)[1])

    loop(1, nq, lambda o: xa_copy(o).start())

    def mix_back(b):
        at = pl.ds(b * chunk * L, chunk * L)
        acc = sum(
            lax.dot_general(
                grad[k, at, :].astype(BF16), w[k], (((1,), (1,)), ((), ())),
                preferred_element_type=F32,
            )
            for k in range(K)
        )
        sg_v[pl.ds(b * chunk, chunk)] = acc.reshape(chunk, L, chans).astype(BF16)

    loop(0, rows // chunk, mix_back)
    sg_copy = pltpu.make_async_copy(sg_v, sgrad_out, out_sem.at[1])
    sg_copy.start()

    loop(1, nq, lambda o: xa_copy(o).wait_recv())
    swap = remote(fin.at[core], fin.at[core], fc_sem.at[0], fc_sem.at[1], partner)
    swap.start()
    half_rows = per_core * chans

    def expand(c):
        wg_v[pl.ds(pl.multiple_of(c * half_rows, 8), half_rows), :] = (
            fin[c].reshape(half_rows, chans).astype(F32)
        )

    expand(core)
    swap.wait()
    expand(1 - core)
    wg_copy = pltpu.make_async_copy(wg_v, wgrad_out, out_sem.at[2])
    wg_copy.start()

    for copy in sig_halo + cot_halo:
        copy.wait_send()
    to_core.wait_send()
    loop(1, nq, lambda o: xy_copy(o).wait_send())
    loop(1, zn, lambda d: z_copy(d).wait_send())
    loop(0, owners - 1, lambda i: za_copy(i).wait_send())
    loop(1, nq, lambda o: xa_copy(o).wait_send())
    conv_copy.wait()
    sg_copy.wait()
    wg_copy.wait()


def prepare(band_kernel, cycle_kernel, support_width, rows):
    lat, nlat = lax.axis_index("lat"), lax.axis_size("lat")
    total = rows * nlat
    first = lat * rows
    kernel_rows = lax.dynamic_slice_in_dim(
        jnp.pad(band_kernel, ((0, 0), (R, R), (0, 0), (0, 0))), first, rows + 2 * R, 1
    ).astype(F32)
    width = lax.dynamic_slice_in_dim(jnp.pad(support_width, (R, R)), first, rows + 2 * R, 0)
    ids = first - R + jnp.arange(rows + 2 * R, dtype=jnp.int32)
    offsets = jnp.abs(jnp.arange(2 * H + 1, dtype=jnp.int32) - H)
    allowed = (offsets[None, :] <= width[:, None]) & ((ids >= P_SIZE) & (ids < total - P_SIZE))[:, None]
    coeffs = jnp.where(allowed[None, :, None, :], kernel_rows, 0.0)
    grown = jnp.pad(coeffs, ((0, 0), (0, 0), (0, 0), (0, 3 * L - 2 * H - 1)))
    flipped = jnp.pad(coeffs[..., ::-1], ((0, 0), (0, 0), (0, 0), (0, 3 * L - 2 * H - 1)))
    lanes = ((0, 0), (0, 0), (0, 256 - 9 * L))
    forward = jnp.pad(flipped[:, R : R + rows].reshape(K, rows, 9 * L), lanes)
    backward = jnp.concatenate(
        [grown[:, 2 - r : 2 - r + rows, r] for r in (2, 1, 0)], -1
    )
    backward = jnp.pad(backward, lanes)
    is_top = lat == 0
    pole = lax.dynamic_slice_in_dim(cycle_kernel, jnp.where(is_top, 0, P_SIZE), P_SIZE, 1).astype(F32)
    padded = jnp.pad(pole, ((0, 0), (0, 0), (2, 2), (0, 0)))
    start = jnp.where(is_top, 3, 2)
    cyc = jnp.stack(
        [lax.dynamic_slice_in_dim(padded[:, p], start - p, SLAB, 1) for p in range(P_SIZE)], 2
    )
    cyc = cyc.reshape(K * SLAB * P_SIZE, -1)
    rev = jnp.roll(cyc[:, ::-1], 1, axis=1)
    return forward, backward, rev, cyc


def local(signal, cotangent, weights, band_kernel, cycle_kernel, support_width):
    rows, _, chans = signal.shape
    nlat, nlon = lax.axis_size("lat"), lax.axis_size("lon")
    ys, zn = nlat // X_LO, nlon // (2 * X_HI)
    nq, owners = XS * ys, zn // 2
    circle = nlon * L
    blocks, cells = rows // 8, rows * L
    piece = K * chans // (2 * nq)
    tiles = piece * chans // (owners * 8 * 128)
    forward, backward, rev, cyc = prepare(band_kernel, cycle_kernel, support_width, rows)
    dma = pltpu.SemaphoreType.DMA
    ext = (rows + 2, L, chans)
    half_rows = K * chans // 2
    scratch = (
        [pltpu.VMEM(ext, BF16)] * 6
        + [pltpu.VMEM(weights.shape, BF16), pltpu.VMEM(forward.shape, F32)]
        + [pltpu.VMEM(backward.shape, F32), pltpu.VMEM(rev.shape, F32), pltpu.VMEM(cyc.shape, F32)]
        + [pltpu.VMEM((blocks, K * 64, 256), BF16)] * 2
        + [pltpu.VMEM((K, cells, chans), BF16), pltpu.VMEM((K, cells, chans), F32)]
        + [pltpu.VMEM((cells, chans), BF16)]
        + [pltpu.VMEM((rows, L, chans), BF16)] * 2
        + [pltpu.VMEM((SLAB + P_SIZE, X_HI, zn, 2, L, chans), BF16)]
        + [pltpu.VMEM((K * P_SIZE * L, SLAB * circle), BF16)]
        + [pltpu.VMEM((K * SLAB * L, P_SIZE * circle), BF16)]
        + [pltpu.VMEM((half_rows, chans), F32)]
        + [pltpu.VMEM((half_rows, chans), BF16)] * 2
        + [pltpu.VMEM((nq, piece, chans), F32)]
        + [pltpu.VMEM((nq, piece, chans), BF16)] * 2
        + [pltpu.VMEM((owners, tiles, 8, 128), F32), pltpu.VMEM((zn, tiles, 8, 128), F32)]
        + [pltpu.VMEM((owners, tiles, 8, 128), F32)]
        + [pltpu.VMEM((2, nq, piece, chans), BF16), pltpu.VMEM((K * chans, chans), F32)]
        + [dma((n,)) for n in (
            7, 16, 16, 6, owners, owners, owners, owners, zn, zn,
            2, nq, nq, zn, zn, owners, owners, nq, nq, 2, 3,
        )]
    )
    field = jax.ShapeDtypeStruct(signal.shape, BF16)
    conv, sgrad, wgrad = pl.pallas_call(
        kernel,
        out_shape=(field, field, jax.ShapeDtypeStruct((K * chans, chans), F32)),
        in_specs=[pl.BlockSpec(memory_space=pl.ANY)] * 7,
        out_specs=[pl.BlockSpec(memory_space=pl.ANY)] * 3,
        scratch_shapes=scratch,
        compiler_params=pltpu.CompilerParams(
            collective_id=0, has_side_effects=True, vmem_limit_bytes=48 * 2**20
        ),
        cost_estimate=pl.CostEstimate(flops=10**9, bytes_accessed=4 * 10**6, transcendentals=0),
    )(signal, cotangent, weights, forward, backward, rev, cyc)
    return conv, sgrad, wgrad.reshape(K, chans, chans)


def solution(mesh):
    placed = (P("lat", "lon", None), P("lat", "lon", None), P(), P(), P(), P())
    return jax.shard_map(
        local,
        mesh=mesh,
        in_specs=placed,
        out_specs=(P("lat", "lon", None), P("lat", "lon", None), P()),
        check_vma=False,
    )
```

```python
import functools
import math

import jax
import jax.numpy as jnp
from jax import lax
from jax.experimental import pallas as pl
from jax.experimental.pallas import tpu as pltpu
from jax.sharding import PartitionSpec as P

K = 4
R = 1
H = 8
P_SIZE = 2
L = 8
SLAB = P_SIZE + R
X_HI = 2
X_LO = 2
XS = X_HI * X_LO
MESH = pl.DeviceIdType.MESH
F32 = jnp.float32
BF16 = jnp.bfloat16


def dot(a, b):
    return jnp.dot(a, b, preferred_element_type=F32)


def kernel(
    sig, cot, w_hbm, band_hbm, cycle_hbm, width_hbm,
    conv_out, sgrad_out, wgrad_out,
    s_o, s_l, s_r, c_o, c_l, c_r, w, band, circ, width,
    bf, bb, cyc, rev, amat, bmat, filt, grad, cot2, conv_v, sg_v,
    slab, qf, qb, gp,
    wall, wsend, wrecv, half, xs, xr, zs, zr, za, fin,
    load_sem, halo_ss, halo_rs, own_sem, pc_ss, pc_rs, px_ss, px_rs, pk_ss, pk_rs,
    ps_ss, ps_rs, pb_sem,
    core_sem, x_ss, x_rs, z_ss, z_rs, za_ss, za_rs, xa_ss, xa_rs, fc_sem, out_sem,
):
    rows, _, chans = sig.shape
    nlat, nlon = lax.axis_size("lat"), lax.axis_size("lon")
    ys, zn = nlat // X_LO, nlon // (2 * X_HI)
    lat, lon = lax.axis_index("lat"), lax.axis_index("lon")
    x_lo, y = lat // ys, lat % ys
    x_hi, z, core = lon // (2 * zn), (lon // 2) % zn, lon % 2
    x = x_hi * X_LO + x_lo
    me_q = x * ys + y
    nq = XS * ys
    blocks = rows // 8
    circle = nlon * L
    first_row, total_rows = lat * rows, rows * nlat
    is_top = lat == 0
    is_polar = is_top | (lat == nlat - 1)

    def place(xx, yy, zz, cc):
        return {"lat": (xx % X_LO) * ys + yy, "lon": (xx // X_LO) * (2 * zn) + zz * 2 + cc}

    def reach(o):
        dx, dy = o // ys, o % ys
        return min(dx, XS - dx) + min(dy, ys - dy)

    xy_order = sorted(range(1, nq), key=lambda o: -reach(o))

    def z_offset(i):
        return zn // 2 + (1 - 2 * (i % 2)) * ((i + 1) // 2)

    def xy_peer(o):
        xx, yy = (x + o // ys) % XS, (y + o % ys) % ys
        return xx * ys + yy, place(xx, yy, z, core)

    def z_peer(d):
        zz = (z + d) % zn
        return zz, place(x, y, zz, core)

    def beside(dlat, dlon):
        return {"lat": (lat + dlat + nlat) % nlat, "lon": (lon + dlon + nlon) % nlon}

    partner = place(x, y, z, 1 - core)
    x_other = place((x + X_LO) % XS, y, z, core)

    def remote(src, dst, ss, rs, dev):
        return pltpu.make_async_remote_copy(
            src_ref=src, dst_ref=dst, send_sem=ss, recv_sem=rs, device_id=dev, device_id_type=MESH
        )

    def loop(lo, hi, f):
        def body(i, c):
            f(i)
            return c

        lax.fori_loop(lo, hi, body, 0)

    barrier = pltpu.get_barrier_semaphore()

    def greet(dev):
        pl.semaphore_signal(barrier, inc=1, device_id=dev, device_id_type=MESH)

    loop(0, zn - 1, lambda i: greet(z_peer(z_offset(i))[1]))
    for o in xy_order:
        greet(xy_peer(o)[1])
    for dlat, dlon in ((1, 1), (1, -1), (-1, 1), (-1, -1), (0, 1), (0, -1)):
        greet(beside(dlat, dlon))

    def band_rows(start, n):
        return band_hbm.at[:, :, pl.ds(pl.multiple_of((start + total_rows) % total_rows, 16), n)]

    loads = [
        pltpu.make_async_copy(a, b, load_sem.at[i])
        for i, (a, b) in enumerate((
            (band_rows(first_row - 16, 16), band.at[:, :, pl.ds(0, 16)]),
            (band_rows(first_row, rows), band.at[:, :, pl.ds(16, rows)]),
            (band_rows(first_row + rows, 16), band.at[:, :, pl.ds(rows + 16, 16)]),
            (width_hbm, width),
            (cycle_hbm, circ),
            (sig, s_o.at[pl.ds(1, rows)]),
            (cot, c_o.at[pl.ds(1, rows)]),
            (w_hbm, w),
        ))
    ]
    for copy in loads:
        copy.start()
    pl.semaphore_wait(barrier, 6 + (nq - 1) + (zn - 1))

    slab_at = jnp.where(is_top, 0, rows - SLAB)
    pole_at = jnp.where(is_top, 0, rows - P_SIZE)
    sig_slab = sig.at[pl.ds(slab_at, SLAB)]
    cot_slab = cot.at[pl.ds(pole_at, P_SIZE)]
    sig_rows, cot_rows = pl.ds(0, SLAB), pl.ds(SLAB, P_SIZE)

    def cot_block(zz):
        return slab.at[cot_rows, x_hi, zz, core]

    def sig_block(zz):
        return slab.at[sig_rows, x_hi, zz, core]

    def cot_z(d):
        return remote(cot_slab, cot_block(z), pc_ss.at[d], pc_rs.at[d], z_peer(d)[1])

    def sig_z(d):
        return remote(sig_slab, sig_block(z), ps_ss.at[d], ps_rs.at[d], z_peer(d)[1])

    def cot_x(d):
        blk = cot_block((z - d + zn) % zn)
        return remote(blk, blk, px_ss.at[d], px_rs.at[d], x_other)

    def cot_core(i):
        part = slab.at[cot_rows, jnp.where(i == 0, x_hi, 1 - x_hi), :, core]
        return remote(part, part, pk_ss.at[i], pk_rs.at[i], partner)

    def sig_x():
        part = slab.at[sig_rows, x_hi, :, core]
        return remote(part, part, pb_sem.at[0], pb_sem.at[1], x_other)

    def sig_core():
        part = slab.at[sig_rows, :, :, core]
        return remote(part, part, pb_sem.at[2], pb_sem.at[3], partner)

    own_slab = [
        pltpu.make_async_copy(cot_slab, cot_block(z), own_sem.at[0]),
        pltpu.make_async_copy(sig_slab, sig_block(z), own_sem.at[1]),
    ]

    @pl.when(is_polar)
    def _():
        own_slab[0].start()
        own_slab[1].start()
        loop(0, zn - 1, lambda i: cot_z(z_offset(i)).start())

    def halo_copies(src, own, left, right, n):
        last, first = src.at[pl.ds(rows - 1, 1)], src.at[pl.ds(0, 1)]
        top, bottom = pl.ds(0, 1), pl.ds(rows + 1, 1)
        spec = (
            (last, left.at[top], beside(1, 1)),
            (last, right.at[top], beside(1, -1)),
            (first, left.at[bottom], beside(-1, 1)),
            (first, right.at[bottom], beside(-1, -1)),
            (last, own.at[top], beside(1, 0)),
            (first, own.at[bottom], beside(-1, 0)),
            (src, left.at[pl.ds(1, rows)], beside(0, 1)),
            (src, right.at[pl.ds(1, rows)], beside(0, -1)),
        )
        return [
            remote(a, b, halo_ss.at[n + i], halo_rs.at[n + i], dev)
            for i, (a, b, dev) in enumerate(spec)
        ]

    sig_halo = halo_copies(sig, s_o, s_l, s_r, 0)
    cot_halo = halo_copies(cot, c_o, c_l, c_r, 8)
    for copy in sig_halo + cot_halo:
        copy.start()

    @pl.when(is_polar)
    def _():
        own_slab[0].wait()
        cot_x(0).start()
        loop(0, zn - 1, lambda i: sig_z(z_offset(i)).start())

    for copy in loads[:4]:
        copy.wait()
    lanes = 256
    lag = lax.broadcasted_iota(jnp.int32, (2 * H + 1, lanes), 0)
    lane = lax.broadcasted_iota(jnp.int32, (2 * H + 1, lanes), 1)
    taps = range(2 * R + 1)
    table_f = [(lane == r * 3 * L + 2 * H - lag).astype(F32).astype(BF16) for r in taps]
    table_b = [(lane == (2 * R - r) * 3 * L + lag).astype(F32).astype(BF16) for r in taps]
    for k in range(K):
        taken = [band[r, k].astype(F32) for r in taps]
        bf[k] = sum(dot(taken[r][16 : 16 + rows].astype(BF16), table_f[r]) for r in taps)
        bb[k] = sum(
            dot(taken[r][17 - r : 17 - r + rows].astype(BF16), table_b[r]) for r in taps
        )
    lane_row = lax.broadcasted_iota(jnp.int32, (1, lanes), 1)
    slot = lane_row // (3 * L)
    away = jnp.abs(lane_row - slot * (3 * L) - H)

    def width_of(i):
        row = first_row + i
        held = width[(row + total_rows) % total_rows]
        return jnp.where((row >= P_SIZE) & (row < total_rows - P_SIZE), held, -1)

    def build(src, dst, backward):
        def block(b):
            allowed = []
            for i in range(8):
                row = b * 8 + i
                if backward:
                    near = [width_of(row + s - R) for s in taps]
                    limit = jnp.where(slot == 0, near[0], jnp.where(slot == 1, near[1], near[2]))
                else:
                    limit = width_of(row)
                allowed.append(away <= limit)
            for k in range(K):
                tile = src[k, pl.ds(pl.multiple_of(b * 8, 8), 8), :]
                for i in range(0, 8, 2):
                    parts = [
                        pltpu.roll(
                            jnp.broadcast_to(jnp.where(allowed[j], tile[j : j + 1], 0.0), (L, lanes)),
                            j * 3 * L, 1, stride=1, stride_axis=0,
                        )
                        for j in (i, i + 1)
                    ]
                    dst[b, pl.ds((k * 8 + i) * L, 2 * L), :] = jnp.concatenate(parts, 0).astype(BF16)

        loop(0, blocks, block)

    def window(o, left, right, b):
        at = pl.ds(b * 8, 10)
        parts = [ref[at].astype(F32) for ref in (left, o, right)]
        both = jnp.concatenate(parts, 1).reshape(30 * L, chans)
        return jnp.concatenate([both, jnp.zeros((2 * L, chans), F32)], 0).astype(BF16)

    build(bf, amat, False)

    loads[4].wait()

    def cycle_rows(src, r):
        row = jnp.broadcast_to(src[r : r + 1, :], (L, circle))
        return pltpu.roll(row, 0, 1, stride=1, stride_axis=0)

    @pl.when(is_polar)
    def _():
        none = jnp.zeros((1, circle), F32)
        for k in range(K):
            for p in range(P_SIZE):

                def tap(r):
                    if not 0 <= r <= 2 * R:
                        return none
                    held = circ[k, r].astype(F32)
                    return jnp.where(is_top, held[p : p + 1], held[P_SIZE + p : P_SIZE + p + 1])

                for r in taps:
                    at = (k * SLAB + r) * P_SIZE + p
                    cyc[at : at + 1, :] = jnp.where(is_top, tap(r - p + R), tap(r - p))
        start = cyc[...]
        from_lag = lax.broadcasted_iota(jnp.int32, (circle, circle), 0)
        to_lag = lax.broadcasted_iota(jnp.int32, (circle, circle), 1)
        turned = ((from_lag + to_lag) % circle == 0).astype(F32).astype(BF16)
        rev[...] = pltpu.roll(dot(start.astype(BF16), turned), lon * L, 1)
        cyc[...] = pltpu.roll(start, lon * L, 1)
        for kj in range(0, K * SLAB, 2):
            for p in range(P_SIZE):
                rows_b = [cycle_rows(cyc, (kj + t) * P_SIZE + p) for t in range(2)]
                qb[pl.ds(kj * L, 16), pl.ds(p * circle, circle)] = jnp.concatenate(rows_b, 0).astype(BF16)

        def pass_on(i):
            d = z_offset(zn - 2 - i)
            cot_z(d).wait_recv()
            cot_x(d).start()

        loop(0, zn - 1, pass_on)
        cot_core(0).start()

    loads[5].wait()
    for copy in sig_halo:
        copy.wait_recv()

    def forward(b):
        part = dot(amat[b], window(s_o, s_l, s_r, b)).astype(BF16)
        for k in range(K):
            filt[k, pl.ds(b * 64, 64), :] = part[k * 64 : (k + 1) * 64]

    loop(0, blocks, forward)
    loads[6].wait()

    def fold(b):
        cot2[pl.ds(b * 64, 64), :] = (
            c_o[pl.ds(1 + b * 8, 8)].astype(F32).reshape(64, chans).astype(BF16)
        )

    loop(0, blocks, fold)

    @pl.when(is_polar)
    def _():
        loop(0, zn, lambda d: cot_x(d).wait_recv())
        cot_core(1).start()

    for k in range(K):
        wall[pl.ds(k * chans, chans), :] = lax.dot_general(
            filt[k], cot2[...], (((0,), (0,)), ((), ())), preferred_element_type=F32
        )

    def circle_of(r):
        return slab[r].astype(F32).reshape(circle, chans).astype(BF16)

    @pl.when(is_polar)
    def _():
        cot_core(0).wait_recv()
        cot_core(1).wait_recv()
        gp[...] = sum(
            dot(qb[:, p * circle : (p + 1) * circle], circle_of(SLAB + p)) for p in range(P_SIZE)
        )
        near = s_o[pl.ds(slab_at + 1, SLAB)].astype(F32).reshape(SLAB * L, chans).astype(BF16)
        for k in range(K):
            wall[pl.ds(k * chans, chans), :] += lax.dot_general(
                near, gp[k * SLAB * L : (k + 1) * SLAB * L].astype(BF16),
                (((0,), (0,)), ((), ())), preferred_element_type=F32,
            )

    half_rows = K * chans // 2
    wsend[...] = wall[pl.ds(pl.multiple_of((1 - core) * half_rows, 8), half_rows), :].astype(BF16)
    to_core = remote(wsend, wrecv, core_sem.at[0], core_sem.at[1], partner)
    to_core.start()
    piece = half_rows // nq
    mine = wall[pl.ds(pl.multiple_of(core * half_rows, 8), half_rows), :]
    to_core.wait_recv()
    summed = mine + wrecv[...].astype(F32)
    half[...] = summed.reshape(nq, piece, chans)
    xs[...] = summed.astype(BF16).reshape(nq, piece, chans)

    def xy_copy(o):
        q, dev = xy_peer(o)
        return remote(xs.at[q], xr.at[o], x_ss.at[o], x_rs.at[o], dev)

    for o in xy_order:
        xy_copy(o).start()

    loads[7].wait()
    chunk = 8

    def mix_out(b):
        at = pl.ds(b * chunk * L, chunk * L)
        acc = sum(dot(filt[k, at, :], w[k]) for k in range(K))
        conv_v[pl.ds(b * chunk, chunk)] = acc.reshape(chunk, L, chans).astype(BF16)

    loop(0, rows // chunk, mix_out)
    build(bb, bmat, True)

    loop(1, nq, lambda o: xy_copy(o).wait_recv())
    total = half[me_q]
    for o in range(1, nq):
        total = total + xr[o].astype(F32)

    for p in range(4):
        zs[p] = total[
            (p // 2) * (piece // 2) : (p // 2 + 1) * (piece // 2), (p % 2) * 128 : (p % 2 + 1) * 128
        ].astype(BF16)

    def z_copy(d):
        zz, dev = z_peer(d)
        return remote(zs.at[zz % 4], zr.at[z], z_ss.at[d], z_rs.at[d], dev)

    loop(0, zn - 1, lambda i: z_copy(z_offset(i)).start())
    zr[z] = zs[z % 4]

    @pl.when(is_polar)
    def _():
        own_slab[1].wait()
        loop(0, zn - 1, lambda i: sig_z(z_offset(i)).wait_recv())
        sig_x().start()

    for copy in cot_halo:
        copy.wait_recv()

    def backward(b):
        part = dot(bmat[b], window(c_o, c_l, c_r, b))
        for k in range(K):
            grad[k, pl.ds(b * 64, 64), :] = part[k * 64 : (k + 1) * 64]

    loop(0, blocks, backward)

    @pl.when(is_polar)
    def _():
        at = pl.multiple_of(slab_at * L, 8)
        for k in range(K):
            grad[k, pl.ds(at, SLAB * L), :] += gp[k * SLAB * L : (k + 1) * SLAB * L]

    def mix_back(b):
        at = pl.ds(b * chunk * L, chunk * L)
        acc = sum(
            lax.dot_general(
                grad[k, at, :].astype(BF16), w[k], (((1,), (1,)), ((), ())),
                preferred_element_type=F32,
            )
            for k in range(K)
        )
        sg_v[pl.ds(b * chunk, chunk)] = acc.reshape(chunk, L, chans).astype(BF16)

    loop(0, rows // chunk, mix_back)
    sg_copy = pltpu.make_async_copy(sg_v, sgrad_out, out_sem.at[1])
    sg_copy.start()

    loop(0, zn - 1, lambda i: z_copy(z_offset(i)).wait_recv())
    acc = zr[0].astype(F32)
    for s in range(1, zn):
        acc = acc + zr[s].astype(F32)
    za[z % 4] = (acc * F32(1.0 / math.sqrt(total_rows * circle))).astype(BF16)
    hand = (2, 1, zn - 1)

    def za_copy(i):
        dst = za.at[z % 4]
        return remote(dst, dst, za_ss.at[i], za_rs.at[i], z_peer(hand[i])[1])

    for i in range(3):
        za_copy(i).start()

    @pl.when(is_polar)
    def _():
        sig_x().wait_recv()
        sig_core().start()

    for i in range(3):
        za_copy(i).wait_recv()
    lines = [jnp.concatenate([za[2 * i].astype(F32), za[2 * i + 1].astype(F32)], 1) for i in range(2)]
    fin[core, me_q] = jnp.concatenate(lines, 0).astype(BF16)

    def xa_copy(o):
        dst = fin.at[core, me_q]
        return remote(dst, dst, xa_ss.at[o], xa_rs.at[o], xy_peer(o)[1])

    for o in xy_order:
        xa_copy(o).start()

    @pl.when(is_polar)
    def _():
        for k in range(K):
            for r in taps:
                at = (k * SLAB + r) * P_SIZE
                rows_f = [cycle_rows(rev, at + p) for p in range(P_SIZE)]
                qf[pl.ds(k * 16, 16), pl.ds(r * circle, circle)] = jnp.concatenate(rows_f, 0).astype(BF16)
        sig_core().wait_recv()
        part = sum(dot(qf[:, r * circle : (r + 1) * circle], circle_of(r)) for r in range(SLAB))
        out = sum(dot(part[k * 16 : (k + 1) * 16].astype(BF16), w[k]) for k in range(K))
        conv_v[pl.ds(pole_at, P_SIZE)] = out.reshape(P_SIZE, L, chans).astype(BF16)

    conv_copy = pltpu.make_async_copy(conv_v, conv_out, out_sem.at[0])
    conv_copy.start()

    loop(1, nq, lambda o: xa_copy(o).wait_recv())
    swap = remote(fin.at[core], fin.at[core], fc_sem.at[0], fc_sem.at[1], partner)
    swap.start()
    wg_copies = [
        pltpu.make_async_copy(fin.at[c], wgrad_out.at[c], out_sem.at[2 + i])
        for i, c in enumerate((core, 1 - core))
    ]
    wg_copies[0].start()

    @pl.when(is_polar)
    def _():
        loop(1, zn, lambda d: cot_z(d).wait_send())
        loop(1, zn, lambda d: sig_z(d).wait_send())
        loop(0, zn, lambda d: cot_x(d).wait_send())
        cot_core(0).wait_send()
        cot_core(1).wait_send()
        sig_x().wait_send()
        sig_core().wait_send()

    for copy in sig_halo + cot_halo:
        copy.wait_send()
    to_core.wait_send()
    loop(1, nq, lambda o: xy_copy(o).wait_send())
    loop(1, zn, lambda d: z_copy(d).wait_send())
    for i in range(3):
        za_copy(i).wait_send()
    loop(1, nq, lambda o: xa_copy(o).wait_send())
    conv_copy.wait()
    sg_copy.wait()
    swap.wait()
    wg_copies[1].start()
    wg_copies[0].wait()
    wg_copies[1].wait()


def local(signal, cotangent, weights, band_kernel, cycle_kernel, support_width):
    rows, _, chans = signal.shape
    nlat, nlon = lax.axis_size("lat"), lax.axis_size("lon")
    ys, zn = nlat // X_LO, nlon // (2 * X_HI)
    nq = XS * ys
    circle = nlon * L
    blocks, cells = rows // 8, rows * L
    half_rows = K * chans // 2
    piece = half_rows // nq
    band = band_kernel.transpose(2, 0, 1, 3)
    cycle = cycle_kernel.transpose(0, 2, 1, 3)
    dma = pltpu.SemaphoreType.DMA
    ext = (rows + 2, L, chans)
    base = pltpu.VMEM((K, rows, 256), F32)
    turns = pltpu.VMEM((K * SLAB * P_SIZE, circle), F32)
    matrices = pltpu.VMEM((blocks, K * 64, 256), BF16)
    scratch = (
        [pltpu.VMEM(ext, BF16)] * 6
        + [pltpu.VMEM(weights.shape, BF16)]
        + [pltpu.VMEM((2 * R + 1, K, rows + 32, 2 * H + 1), BF16)]
        + [pltpu.VMEM((K, 2 * R + 1, 2 * P_SIZE, circle), BF16)]
        + [pltpu.SMEM(support_width.shape, jnp.int32)]
        + [base] * 2 + [turns] * 2 + [matrices] * 2
        + [pltpu.VMEM((K, cells, chans), BF16), pltpu.VMEM((K, cells, chans), F32)]
        + [pltpu.VMEM((cells, chans), BF16)]
        + [pltpu.VMEM((rows, L, chans), BF16)] * 2
        + [pltpu.VMEM((SLAB + P_SIZE, X_HI, zn, 2, L, chans), BF16)]
        + [pltpu.VMEM((K * P_SIZE * L, SLAB * circle), BF16)]
        + [pltpu.VMEM((K * SLAB * L, P_SIZE * circle), BF16)]
        + [pltpu.VMEM((K * SLAB * L, chans), F32)]
        + [pltpu.VMEM((2 * half_rows, chans), F32)]
        + [pltpu.VMEM((half_rows, chans), BF16)] * 2
        + [pltpu.VMEM((nq, piece, chans), F32)]
        + [pltpu.VMEM((nq, piece, chans), BF16)] * 2
        + [pltpu.VMEM((n, piece // 2, 128), BF16) for n in (4, zn, 4)]
        + [pltpu.VMEM((2, nq, piece, chans), BF16)]
        + [dma((n,)) for n in (
            8, 16, 16, 2, zn, zn, zn, zn, 2, 2,
            zn, zn, 4,
            2, nq, nq, zn, zn, 3, 3, nq, nq, 2, 4,
        )]
    )
    field = jax.ShapeDtypeStruct(signal.shape, BF16)
    conv, sgrad, wgrad = pl.pallas_call(
        kernel,
        out_shape=(field, field, jax.ShapeDtypeStruct((2, nq, piece, chans), BF16)),
        in_specs=[pl.BlockSpec(memory_space=pl.ANY)] * 6,
        out_specs=[pl.BlockSpec(memory_space=pl.ANY)] * 3,
        scratch_shapes=scratch,
        compiler_params=pltpu.CompilerParams(
            collective_id=0, has_side_effects=True, vmem_limit_bytes=40 * 2**20
        ),
        cost_estimate=pl.CostEstimate(flops=10**9, bytes_accessed=4 * 10**6, transcendentals=0),
    )(signal, cotangent, weights, band, cycle, support_width)
    return conv, sgrad, wgrad.astype(F32).reshape(K, chans, chans)


def solution(mesh):
    placed = (P("lat", "lon", None), P("lat", "lon", None), P(), P(), P(), P())
    return jax.shard_map(
        local,
        mesh=mesh,
        in_specs=placed,
        out_specs=(P("lat", "lon", None), P("lat", "lon", None), P()),
        check_vma=False,
    )
```

```python
import functools
import math

import jax
import jax.numpy as jnp
from jax import lax
from jax.experimental import pallas as pl
from jax.experimental.pallas import tpu as pltpu
from jax.sharding import PartitionSpec as P

K = 4
R = 1
H = 8
P_SIZE = 2
L = 8
SLAB = P_SIZE + R
X_HI = 2
X_LO = 2
XS = X_HI * X_LO
MESH = pl.DeviceIdType.MESH
F32 = jnp.float32
BF16 = jnp.bfloat16


def dot(a, b):
    return jnp.dot(a, b, preferred_element_type=F32)


def kernel(
    sig, cot, w_hbm, band_hbm, cycle_hbm, width_hbm,
    conv_out, sgrad_out, wgrad_out,
    s_o, s_l, s_r, c_o, c_l, c_r, w, band, circ, width, taps_v, taps_t,
    bf, bb, cyc, rev, amat, bmat, filt, grad, cot2, conv_v, sg_v,
    slab, qf, qb, qt, gw, sw, part_s, part_r, own_part,
    wall, wsend, wrecv, half, xs, xr, zs, zr, za, fin,
    far_sem, load_sem, halo_ss, halo_rs, own_sem, pc_ss, pc_rs, px_ss, px_rs, pk_sem,
    ps_ss, ps_rs, pb_ss, pb_rs, pp_sem,
    core_sem, x_ss, x_rs, z_ss, z_rs, za_ss, za_rs, xa_ss, xa_rs, fc_sem, out_sem,
):
    rows, _, chans = sig.shape
    nlat, nlon = lax.axis_size("lat"), lax.axis_size("lon")
    ys, zn = nlat // X_LO, nlon // (2 * X_HI)
    lat, lon = lax.axis_index("lat"), lax.axis_index("lon")
    x_lo, y = lat // ys, lat % ys
    x_hi, z, core = lon // (2 * zn), (lon // 2) % zn, lon % 2
    x = x_hi * X_LO + x_lo
    me_q = x * ys + y
    nq = XS * ys
    blocks = rows // 8
    circle = nlon * L
    first_row, total_rows = lat * rows, rows * nlat
    is_top = lat == 0
    is_polar = is_top | (lat == nlat - 1)

    def place(xx, yy, zz, cc):
        return {"lat": (xx % X_LO) * ys + yy, "lon": (xx // X_LO) * (2 * zn) + zz * 2 + cc}

    def reach(o):
        dx, dy = o // ys, o % ys
        return min(dx, XS - dx) + min(dy, ys - dy)

    xy_order = sorted(range(1, nq), key=lambda o: -reach(o))

    near, mid = zn // 4, zn // 2

    def z_offset(i):
        return mid + (1 - 2 * (i % 2)) * ((i + 1) // 2)

    near_order = [d for n in range(near, 0, -1) for d in (n, zn - n)]

    def xy_peer(o):
        xx, yy = (x + o // ys) % XS, (y + o % ys) % ys
        return xx * ys + yy, place(xx, yy, z, core)

    def z_peer(d):
        zz = (z + d) % zn
        return zz, place(x, y, zz, core)

    def beside(dlat, dlon):
        return {"lat": (lat + dlat + nlat) % nlat, "lon": (lon + dlon + nlon) % nlon}

    partner = place(x, y, z, 1 - core)
    x_other = place((x + X_LO) % XS, y, z, core)

    def remote(src, dst, ss, rs, dev):
        return pltpu.make_async_remote_copy(
            src_ref=src, dst_ref=dst, send_sem=ss, recv_sem=rs, device_id=dev, device_id_type=MESH
        )

    def loop(lo, hi, f):
        def body(i, c):
            f(i)
            return c

        lax.fori_loop(lo, hi, body, 0)

    barrier = pltpu.get_barrier_semaphore()

    def greet(dev):
        pl.semaphore_signal(barrier, inc=1, device_id=dev, device_id_type=MESH)

    for d in near_order:
        greet(z_peer(d)[1])
    @pl.when(is_polar)
    def _():
        for d in near_order:
            greet(place((x + X_LO) % XS, y, (z + d) % zn, core))

    for o in xy_order:
        greet(xy_peer(o)[1])
    for dlat, dlon in ((1, 1), (1, -1), (-1, 1), (-1, -1), (0, 1), (0, -1)):
        greet(beside(dlat, dlon))

    loads = [
        pltpu.make_async_copy(a, b, load_sem.at[i])
        for i, (a, b) in enumerate((
            (band_hbm, band),
            (width_hbm, width),
            (cycle_hbm, circ),
            (sig, s_o.at[pl.ds(1, rows)]),
            (cot, c_o.at[pl.ds(1, rows)]),
            (w_hbm, w),
        ))
    ]
    for copy in loads:
        copy.start()
    greeted = 6 + (nq - 1) + 2 * near
    pl.semaphore_wait(barrier, jnp.where(is_polar, greeted + 2 * near, greeted))
    for i, d in enumerate((near, zn - near)):
        pl.semaphore_signal(far_sem.at[i], inc=1, device_id=z_peer(d)[1], device_id_type=MESH)

    slab_at = jnp.where(is_top, 0, rows - SLAB)
    pole_at = jnp.where(is_top, 0, rows - P_SIZE)
    sig_slab = sig.at[pl.ds(slab_at, SLAB)]
    cot_slab = cot.at[pl.ds(pole_at, P_SIZE)]
    sig_rows, cot_rows = pl.ds(0, SLAB), pl.ds(SLAB, P_SIZE)

    def seen(d):
        return mid - d if d <= mid else mid + zn - d

    def cot_z(d):
        dst = slab.at[cot_rows, x_hi, seen(d), core]
        return remote(cot_slab, dst, pc_ss.at[d], pc_rs.at[d], z_peer(d)[1])

    def sig_z(d):
        dst = slab.at[sig_rows, x_hi, seen(d), core]
        return remote(sig_slab, dst, ps_ss.at[d], ps_rs.at[d], z_peer(d)[1])

    def cot_x(d):
        dst = slab.at[cot_rows, x_hi, seen(d), core]
        dev = place((x + X_LO) % XS, y, (z + d) % zn, core)
        return remote(cot_slab, dst, px_ss.at[d], px_rs.at[d], dev)

    def cot_core():
        part = slab.at[cot_rows, :, pl.ds(mid - near, 2 * near + 1), core]
        return remote(part, part, pk_sem.at[0], pk_sem.at[1], partner)

    def far_copy(i):
        src, dst, n, d = (
            (mid - near, 0, near, near), (mid + 1, mid + near + 1, near - 1, zn - near)
        )[i]
        return remote(
            slab.at[:, x_hi, pl.ds(src, n), core], slab.at[:, x_hi, pl.ds(dst, n), core],
            ps_ss.at[zn + i], ps_rs.at[zn + i], z_peer(d)[1],
        )

    fars = [0, 1] if near > 1 else [0]
    spans = [(cot_rows, 0, mid - near), (cot_rows, mid + near + 1, mid - near - 1), (sig_rows, 0, zn)]
    spans = [span for span in spans if span[2] > 0]

    def rest_core(i):
        held, lo, n = spans[i]
        part = slab.at[held, x_hi, pl.ds(lo, n), core]
        return remote(part, part, pb_ss.at[i], pb_rs.at[i], partner)

    def part_copy():
        return remote(part_s, part_r, pp_sem.at[0], pp_sem.at[1], x_other)

    own_slab = [
        pltpu.make_async_copy(cot_slab, slab.at[cot_rows, x_hi, mid, core], own_sem.at[0]),
        pltpu.make_async_copy(sig_slab, slab.at[sig_rows, x_hi, mid, core], own_sem.at[1]),
    ]

    @pl.when(is_polar)
    def _():
        own_slab[0].start()
        own_slab[1].start()
        for d in near_order:
            cot_x(d).start()
        for d in near_order:
            cot_z(d).start()
        cot_x(0).start()
        for d in near_order:
            sig_z(d).start()

    def halo_copies(src, own, left, right, n):
        last, first = src.at[pl.ds(rows - 1, 1)], src.at[pl.ds(0, 1)]
        top, bottom = pl.ds(0, 1), pl.ds(rows + 1, 1)
        spec = (
            (last, left.at[top], beside(1, 1)),
            (last, right.at[top], beside(1, -1)),
            (first, left.at[bottom], beside(-1, 1)),
            (first, right.at[bottom], beside(-1, -1)),
            (last, own.at[top], beside(1, 0)),
            (first, own.at[bottom], beside(-1, 0)),
            (src, left.at[pl.ds(1, rows)], beside(0, 1)),
            (src, right.at[pl.ds(1, rows)], beside(0, -1)),
        )
        return [
            remote(a, b, halo_ss.at[n + i], halo_rs.at[n + i], dev)
            for i, (a, b, dev) in enumerate(spec)
        ]

    sig_halo = halo_copies(sig, s_o, s_l, s_r, 0)
    cot_halo = halo_copies(cot, c_o, c_l, c_r, 8)
    for copy in sig_halo + cot_halo:
        copy.start()

    loads[0].wait()
    loads[1].wait()
    lanes = 256
    taps = range(2 * R + 1)
    lags = 2 * H + 1
    used = (2 * R + 1) * lags * K
    taps_v[...] = jnp.zeros_like(taps_v)
    for r in taps:
        for d in range(lags):
            taps_v[pl.ds((r * lags + d) * K, K), :] = band[r, d].astype(F32)
    taps_t[pl.ds(0, 16), :] = jnp.zeros((16, lanes), BF16)
    taps_t[pl.ds(16, total_rows), :] = jnp.transpose(taps_v[...])[:total_rows].astype(BF16)
    taps_t[pl.ds(16 + total_rows, 16), :] = jnp.zeros((16, lanes), BF16)
    mine = taps_t[pl.ds(pl.multiple_of(first_row, 16), rows + 32), :]
    held = lax.broadcasted_iota(jnp.int32, (lanes, 1), 0)
    held_k, held_r, held_d = held % K, held // (K * lags), held // K % lags
    lane = lax.broadcasted_iota(jnp.int32, (lanes, lanes), 1)
    to_f = jnp.where(held < used, held_r * 3 * L + 2 * H - held_d, -1)
    to_b = jnp.where(held < used, (2 * R - held_r) * 3 * L + held_d, -1)
    for k in range(K):
        placed = [
            dot(mine, (lane == jnp.where(held_k == k, to, -1)).astype(F32).astype(BF16))
            for to in (to_f, to_b)
        ]
        bf[k] = placed[0][16 : 16 + rows]
        slots = lax.broadcasted_iota(jnp.int32, (1, lanes), 1) // (3 * L)
        above, same, below = (placed[1][15 + s : 15 + s + rows] for s in taps)
        bb[k] = jnp.where(slots == 0, above, jnp.where(slots == 1, same, below))
    lane_row = lax.broadcasted_iota(jnp.int32, (1, lanes), 1)
    slot = lane_row // (3 * L)
    away = jnp.abs(lane_row - slot * (3 * L) - H)

    def width_of(i):
        row = first_row + i
        held = width[(row + total_rows) % total_rows]
        return jnp.where((row >= P_SIZE) & (row < total_rows - P_SIZE), held, -1)

    def build(src, dst, backward):
        def block(b):
            allowed = []
            for i in range(8):
                row = b * 8 + i
                if backward:
                    near = [width_of(row + s - R) for s in taps]
                    limit = jnp.where(slot == 0, near[0], jnp.where(slot == 1, near[1], near[2]))
                else:
                    limit = width_of(row)
                allowed.append(away <= limit)
            for k in range(K):
                tile = src[k, pl.ds(pl.multiple_of(b * 8, 8), 8), :]
                for i in range(0, 8, 2):
                    parts = [
                        pltpu.roll(
                            jnp.broadcast_to(jnp.where(allowed[j], tile[j : j + 1], 0.0), (L, lanes)),
                            j * 3 * L, 1, stride=1, stride_axis=0,
                        )
                        for j in (i, i + 1)
                    ]
                    dst[b, pl.ds((k * 8 + i) * L, 2 * L), :] = jnp.concatenate(parts, 0).astype(BF16)

        loop(0, blocks, block)

    def window(o, left, right, b):
        at = pl.ds(b * 8, 10)
        parts = [ref[at].astype(F32) for ref in (left, o, right)]
        both = jnp.concatenate(parts, 1).reshape(30 * L, chans)
        return jnp.concatenate([both, jnp.zeros((2 * L, chans), F32)], 0).astype(BF16)

    build(bf, amat, False)

    loads[2].wait()

    def cycle_rows(src, r):
        row = jnp.broadcast_to(src[r : r + 1, :], (L, circle))
        return pltpu.roll(row, 0, 1, stride=1, stride_axis=0)

    @pl.when(is_polar)
    def _():
        none = jnp.zeros((1, circle), F32)
        for k in range(K):
            for p in range(P_SIZE):

                def tap(r):
                    if not 0 <= r <= 2 * R:
                        return none
                    held = circ[k, r].astype(F32)
                    return jnp.where(is_top, held[p : p + 1], held[P_SIZE + p : P_SIZE + p + 1])

                for r in taps:
                    at = (k * SLAB + r) * P_SIZE + p
                    cyc[at : at + 1, :] = jnp.where(is_top, tap(r - p + R), tap(r - p))
        col = lax.broadcasted_iota(jnp.int32, (1, circle), 1)
        t, c = col // (8 * L) - near, col % (8 * L)
        xh, o, cc, l = c // (4 * L), c // (2 * L) % 2, c // L % 2, c % L
        z_cot, z_sig = (z + t + o + zn) % zn, (z - t + zn) % zn
        lag = (xh - x_hi) * (circle // 2) + (z_cot - z_sig) * (2 * L) + (cc - core) * L + l
        lag = (lag + 2 * circle) % circle
        pick = (lax.broadcasted_iota(jnp.int32, (circle, circle), 0) == lag).astype(F32).astype(BF16)
        for p in range(P_SIZE):
            turned = [cycle_rows(cyc, n * P_SIZE + p) for n in range(K * SLAB)]
            qt[p] = dot(jnp.concatenate(turned, 0).astype(BF16), pick).astype(BF16)
        own_slab[0].wait()
        for d in near_order:
            cot_z(d).wait_recv()
        for d in [0] + near_order:
            cot_x(d).wait_recv()
        cot_core().start()

    loads[3].wait()
    for copy in sig_halo:
        copy.wait_recv()

    def forward(b):
        part = dot(amat[b], window(s_o, s_l, s_r, b)).astype(BF16)
        for k in range(K):
            filt[k, pl.ds(b * 64, 64), :] = part[k * 64 : (k + 1) * 64]

    loop(0, blocks, forward)
    loads[4].wait()

    def fold(b):
        cot2[pl.ds(b * 64, 64), :] = (
            c_o[pl.ds(1 + b * 8, 8)].astype(F32).reshape(64, chans).astype(BF16)
        )

    loop(0, blocks, fold)

    for k in range(K):
        wall[pl.ds(k * chans, chans), :] = lax.dot_general(
            filt[k], cot2[...], (((0,), (0,)), ((), ())), preferred_element_type=F32
        )

    def cells(ref):
        held = ref.astype(F32)
        return held.reshape(-1, chans)

    @pl.when(is_polar)
    def _():
        own_slab[1].wait()
        for d in near_order:
            sig_z(d).wait_recv()
        cot_core().wait_recv()
        for i in range(2 * near):
            t = i - near
            turned = sum(
                dot(
                    qt[p, :, i * 8 * L : (i + 1) * 8 * L],
                    cells(slab[SLAB + p, :, mid + t : mid + t + 2]).astype(BF16),
                )
                for p in range(P_SIZE)
            )
            for k in range(K):
                gw[k, pl.ds(i * SLAB * L, SLAB * L), :] = turned[k * SLAB * L : (k + 1) * SLAB * L]
            sw[pl.ds(i * SLAB * L, SLAB * L), :] = cells(slab[0:SLAB, x_hi, mid - t, core])
        for k in range(K):
            wall[pl.ds(k * chans, chans), :] += lax.dot_general(
                sw[...].astype(BF16), gw[k].astype(BF16),
                (((0,), (0,)), ((), ())), preferred_element_type=F32,
            )

    half_rows = K * chans // 2
    wsend[...] = wall[pl.ds(pl.multiple_of((1 - core) * half_rows, 8), half_rows), :].astype(BF16)
    to_core = remote(wsend, wrecv, core_sem.at[0], core_sem.at[1], partner)
    to_core.start()
    piece = half_rows // nq
    mine = wall[pl.ds(pl.multiple_of(core * half_rows, 8), half_rows), :]
    to_core.wait_recv()
    summed = mine + wrecv[...].astype(F32)
    half[...] = summed.reshape(nq, piece, chans)
    xs[...] = summed.astype(BF16).reshape(nq, piece, chans)

    def xy_copy(o):
        q, dev = xy_peer(o)
        return remote(xs.at[q], xr.at[o], x_ss.at[o], x_rs.at[o], dev)

    for o in xy_order:
        xy_copy(o).start()

    @pl.when(is_polar)
    def _():
        for i in fars:
            far_copy(i).start()

    for i in range(2):
        pl.semaphore_wait(far_sem.at[i], 1)

    loads[5].wait()
    chunk = 8

    def mix_out(b):
        at = pl.ds(b * chunk * L, chunk * L)
        acc = sum(dot(filt[k, at, :], w[k]) for k in range(K))
        conv_v[pl.ds(b * chunk, chunk)] = acc.reshape(chunk, L, chans).astype(BF16)

    loop(0, rows // chunk, mix_out)
    build(bb, bmat, True)

    for copy in cot_halo:
        copy.wait_recv()

    def backward(b):
        part = dot(bmat[b], window(c_o, c_l, c_r, b))
        for k in range(K):
            grad[k, pl.ds(b * 64, 64), :] = part[k * 64 : (k + 1) * 64]

    loop(0, blocks, backward)

    loop(1, nq, lambda o: xy_copy(o).wait_recv())
    total = half[me_q]
    for o in range(1, nq):
        total = total + xr[o].astype(F32)

    for p in range(4):
        zs[p] = total[
            (p // 2) * (piece // 2) : (p // 2 + 1) * (piece // 2), (p % 2) * 128 : (p % 2 + 1) * 128
        ].astype(BF16)

    def z_copy(d):
        zz, dev = z_peer(d)
        return remote(zs.at[zz % 4], zr.at[z], z_ss.at[d], z_rs.at[d], dev)

    loop(0, zn - 1, lambda i: z_copy(z_offset(i)).start())
    zr[z] = zs[z % 4]

    @pl.when(is_polar)
    def _():
        for i in fars:
            far_copy(i).wait_recv()
        for i in range(len(spans)):
            rest_core(i).start()

    def mix_back(b):
        at = pl.ds(b * chunk * L, chunk * L)
        acc = sum(
            lax.dot_general(
                grad[k, at, :].astype(BF16), w[k], (((1,), (1,)), ((), ())),
                preferred_element_type=F32,
            )
            for k in range(K)
        )
        sg_v[pl.ds(b * chunk, chunk)] = acc.reshape(chunk, L, chans).astype(BF16)

    loop(0, rows // chunk, mix_back)

    @pl.when(is_polar)
    def _():
        start = cyc[...]
        from_lag = lax.broadcasted_iota(jnp.int32, (circle, circle), 0)
        to_lag = lax.broadcasted_iota(jnp.int32, (circle, circle), 1)
        turned = ((from_lag + to_lag) % circle == 0).astype(F32).astype(BF16)
        rev[...] = pltpu.roll(dot(start.astype(BF16), turned), lon * L, 1)
        cyc[...] = pltpu.roll(start, lon * L, 1)
        side = circle // 2
        shift = (side + (mid - z) * 2 * L) % side

        def circulant(src, rows_of, dst, at):
            full = jnp.concatenate([cycle_rows(src, n) for n in rows_of], 0)
            for h in range(2):
                turned_side = pltpu.roll(full[:, h * side : (h + 1) * side], shift, 1)
                dst[h, :, pl.ds(at, side)] = turned_side.astype(BF16)

        for p in range(P_SIZE):
            circulant(cyc, [n * P_SIZE + p for n in range(K * SLAB)], qb, p * side)
        for r in taps:
            circulant(
                rev, [(k * SLAB + r) * P_SIZE + p for k in range(K) for p in range(P_SIZE)], qf, r * side
            )

        for i in range(len(spans)):
            rest_core(i).wait_recv()
        held_rows = [cells(slab[r, x_hi]).astype(BF16) for r in range(SLAB + P_SIZE)]

        def share(h):
            front = sum(dot(qf[h, :, r * side : (r + 1) * side], held_rows[r]) for r in range(SLAB))
            back = sum(
                dot(qb[h, :, p * side : (p + 1) * side], held_rows[SLAB + p]) for p in range(P_SIZE)
            )
            return jnp.concatenate([front, back], 0)

        part_s[...] = share(1 - x_hi).astype(BF16)
        part_copy().start()
        own_part[...] = share(x_hi)

    loop(0, zn - 1, lambda i: z_copy(z_offset(i)).wait_recv())
    acc = zr[0].astype(F32)
    for s in range(1, zn):
        acc = acc + zr[s].astype(F32)
    za[z % 4] = (acc * F32(1.0 / math.sqrt(total_rows * circle))).astype(BF16)
    hand = (2, 1, zn - 1)

    def za_copy(i):
        dst = za.at[z % 4]
        return remote(dst, dst, za_ss.at[i], za_rs.at[i], z_peer(hand[i])[1])

    for i in range(3):
        za_copy(i).start()

    for i in range(3):
        za_copy(i).wait_recv()
    lines = [jnp.concatenate([za[2 * i].astype(F32), za[2 * i + 1].astype(F32)], 1) for i in range(2)]
    fin[core, me_q] = jnp.concatenate(lines, 0).astype(BF16)

    def xa_copy(o):
        dst = fin.at[core, me_q]
        return remote(dst, dst, xa_ss.at[o], xa_rs.at[o], xy_peer(o)[1])

    for o in xy_order:
        xa_copy(o).start()

    @pl.when(is_polar)
    def _():
        part_copy().wait_recv()
        sums = own_part[...] + part_r[...].astype(F32)
        front, extra = sums[: K * P_SIZE * L], sums[K * P_SIZE * L :]
        out = sum(dot(front[k * 16 : (k + 1) * 16].astype(BF16), w[k]) for k in range(K))
        conv_v[pl.ds(pole_at, P_SIZE)] = out.reshape(P_SIZE, L, chans).astype(BF16)
        at = pl.multiple_of(slab_at * L, 8)
        back = sum(
            lax.dot_general(
                (grad[k, pl.ds(at, SLAB * L), :] + extra[k * SLAB * L : (k + 1) * SLAB * L]).astype(BF16),
                w[k], (((1,), (1,)), ((), ())), preferred_element_type=F32,
            )
            for k in range(K)
        )
        sg_v[pl.ds(slab_at, SLAB)] = back.reshape(SLAB, L, chans).astype(BF16)

    sg_copy = pltpu.make_async_copy(sg_v, sgrad_out, out_sem.at[1])
    sg_copy.start()
    conv_copy = pltpu.make_async_copy(conv_v, conv_out, out_sem.at[0])
    conv_copy.start()

    loop(1, nq, lambda o: xa_copy(o).wait_recv())
    swap = remote(fin.at[core], fin.at[core], fc_sem.at[0], fc_sem.at[1], partner)
    swap.start()
    wg_copies = [
        pltpu.make_async_copy(fin.at[c], wgrad_out.at[c], out_sem.at[2 + i])
        for i, c in enumerate((core, 1 - core))
    ]
    wg_copies[0].start()

    @pl.when(is_polar)
    def _():
        for d in near_order:
            cot_z(d).wait_send()
            sig_z(d).wait_send()
        for d in [0] + near_order:
            cot_x(d).wait_send()
        cot_core().wait_send()
        for i in fars:
            far_copy(i).wait_send()
        for i in range(len(spans)):
            rest_core(i).wait_send()
        part_copy().wait_send()

    for copy in sig_halo + cot_halo:
        copy.wait_send()
    to_core.wait_send()
    loop(1, nq, lambda o: xy_copy(o).wait_send())
    loop(1, zn, lambda d: z_copy(d).wait_send())
    for i in range(3):
        za_copy(i).wait_send()
    loop(1, nq, lambda o: xa_copy(o).wait_send())
    conv_copy.wait()
    sg_copy.wait()
    swap.wait()
    wg_copies[1].start()
    wg_copies[0].wait()
    wg_copies[1].wait()


def finish(conv, sgrad, wgrad):
    parts = 4

    def body(conv_in, sg_in, wg_in, conv_out, sg_out, wg_out, held, wide, fields, sems):
        ends = [(conv_in, fields.at[0], conv_out), (sg_in, fields.at[1], sg_out)]
        ends += [(wg_in.at[k], held.at[k], wg_out.at[k]) for k in range(parts)]
        loads = [pltpu.make_async_copy(a, b, sems.at[0, i]) for i, (a, b, _) in enumerate(ends)]
        stores = [
            pltpu.make_async_copy(b if i < 2 else wide.at[i - 2], c, sems.at[1, i])
            for i, (_, b, c) in enumerate(ends)
        ]
        for copy in loads:
            copy.start()
        for i in range(2 + parts):
            loads[i].wait()
            if i >= 2:
                wide[i - 2] = held[i - 2].astype(F32)
            stores[i].start()
        for copy in stores:
            copy.wait()

    return pl.pallas_call(
        body,
        out_shape=(
            jax.ShapeDtypeStruct(conv.shape, conv.dtype),
            jax.ShapeDtypeStruct(sgrad.shape, sgrad.dtype),
            jax.ShapeDtypeStruct(wgrad.shape, F32),
        ),
        in_specs=[pl.BlockSpec(memory_space=pl.ANY)] * 3,
        out_specs=[pl.BlockSpec(memory_space=pl.ANY)] * 3,
        scratch_shapes=[
            pltpu.VMEM(wgrad.shape, BF16), pltpu.VMEM(wgrad.shape, F32),
            pltpu.VMEM((2,) + conv.shape, BF16), pltpu.SemaphoreType.DMA((2, 2 + parts)),
        ],
        compiler_params=pltpu.CompilerParams(vmem_limit_bytes=60 * 2**20),
    )(conv, sgrad, wgrad)


def local(signal, cotangent, weights, band_kernel, cycle_kernel, support_width):
    rows, _, chans = signal.shape
    nlat, nlon = lax.axis_size("lat"), lax.axis_size("lon")
    ys, zn = nlat // X_LO, nlon // (2 * X_HI)
    nq = XS * ys
    circle = nlon * L
    blocks, cells = rows // 8, rows * L
    half_rows = K * chans // 2
    piece = half_rows // nq
    band = band_kernel.transpose(2, 3, 0, 1)
    cycle = cycle_kernel.transpose(0, 2, 1, 3)
    dma = pltpu.SemaphoreType.DMA
    ext = (rows + 2, L, chans)
    base = pltpu.VMEM((K, rows, 256), F32)
    turns = pltpu.VMEM((K * SLAB * P_SIZE, circle), F32)
    matrices = pltpu.VMEM((blocks, K * 64, 256), BF16)
    scratch = (
        [pltpu.VMEM(ext, BF16)] * 6
        + [pltpu.VMEM(weights.shape, BF16)]
        + [pltpu.VMEM(band.shape, BF16)]
        + [pltpu.VMEM((K, 2 * R + 1, 2 * P_SIZE, circle), BF16)]
        + [pltpu.SMEM(support_width.shape, jnp.int32)]
        + [pltpu.VMEM((256, rows * nlat), F32), pltpu.VMEM((rows * nlat + 32, 256), BF16)]
        + [base] * 2 + [turns] * 2 + [matrices] * 2
        + [pltpu.VMEM((K, cells, chans), BF16), pltpu.VMEM((K, cells, chans), F32)]
        + [pltpu.VMEM((cells, chans), BF16)]
        + [pltpu.VMEM((rows, L, chans), BF16)] * 2
        + [pltpu.VMEM((SLAB + P_SIZE, X_HI, zn, 2, L, chans), BF16)]
        + [pltpu.VMEM((2, K * P_SIZE * L, SLAB * circle // 2), BF16)]
        + [pltpu.VMEM((2, K * SLAB * L, P_SIZE * circle // 2), BF16)]
        + [pltpu.VMEM((P_SIZE, K * SLAB * L, circle), BF16)]
        + [pltpu.VMEM((K, zn // 2 * SLAB * L, chans), F32), pltpu.VMEM((zn // 2 * SLAB * L, chans), F32)]
        + [pltpu.VMEM((K * (P_SIZE + SLAB) * L, chans), BF16)] * 2
        + [pltpu.VMEM((K * (P_SIZE + SLAB) * L, chans), F32)]
        + [pltpu.VMEM((2 * half_rows, chans), F32)]
        + [pltpu.VMEM((half_rows, chans), BF16)] * 2
        + [pltpu.VMEM((nq, piece, chans), F32)]
        + [pltpu.VMEM((nq, piece, chans), BF16)] * 2
        + [pltpu.VMEM((n, piece // 2, 128), BF16) for n in (4, zn, 4)]
        + [pltpu.VMEM((2, nq, piece, chans), BF16)]
        + [pltpu.SemaphoreType.REGULAR((2,))]
        + [dma((n,)) for n in (
            6, 16, 16, 2, zn, zn, zn, zn, 2,
            zn + 2, zn + 2, 3, 3, 2,
            2, nq, nq, zn, zn, 3, 3, nq, nq, 2, 4,
        )]
    )
    field = jax.ShapeDtypeStruct(signal.shape, BF16)
    conv, sgrad, wgrad = pl.pallas_call(
        kernel,
        out_shape=(field, field, jax.ShapeDtypeStruct((2, nq, piece, chans), BF16)),
        in_specs=[pl.BlockSpec(memory_space=pl.ANY)] * 6,
        out_specs=[pl.BlockSpec(memory_space=pl.ANY)] * 3,
        scratch_shapes=scratch,
        compiler_params=pltpu.CompilerParams(
            collective_id=0, has_side_effects=True, vmem_limit_bytes=60 * 2**20
        ),
        cost_estimate=pl.CostEstimate(flops=10**9, bytes_accessed=4 * 10**6, transcendentals=0),
    )(signal, cotangent, weights, band, cycle, support_width)
    return finish(conv, sgrad, wgrad.reshape(K, chans, chans))


def solution(mesh):
    placed = (P("lat", "lon", None), P("lat", "lon", None), P(), P(), P(), P())
    return jax.shard_map(
        local,
        mesh=mesh,
        in_specs=placed,
        out_specs=(P("lat", "lon", None), P("lat", "lon", None), P()),
        check_vma=False,
    )
```

```python
import functools
import math

import jax
import jax.numpy as jnp
from jax import lax
from jax.experimental import pallas as pl
from jax.experimental.pallas import tpu as pltpu
from jax.sharding import PartitionSpec as P

K = 4
R = 1
H = 8
P_SIZE = 2
L = 8
SLAB = P_SIZE + R
X_HI = 2
X_LO = 2
XS = X_HI * X_LO
MESH = pl.DeviceIdType.MESH
F32 = jnp.float32
BF16 = jnp.bfloat16


def dot(a, b):
    return jnp.dot(a, b, preferred_element_type=F32)


def kernel(
    sig, cot, w_hbm, band_hbm, cycle_hbm, width_hbm,
    conv_out, sgrad_out, wgrad_out,
    s_o, s_l, s_r, c_o, c_l, c_r, w, band, circ, width, taps_v, taps_t,
    bf, bb, cyc, rev, amat, bmat, filt, grad, cot2, conv_v, sg_v,
    slab, qf, qb, qt, gw, sw, part_s, part_r, own_part,
    wall, wsend, wrecv, half, xs, xr, zs, zr, za, fin,
    far_sem, load_sem, halo_ss, halo_rs, own_sem, pc_ss, pc_rs, px_ss, px_rs, pk_sem,
    ps_ss, ps_rs, pb_ss, pb_rs, pp_sem,
    core_sem, x_ss, x_rs, z_ss, z_rs, za_ss, za_rs, xa_ss, xa_rs, fc_ss, fc_rs, out_sem,
):
    rows, _, chans = sig.shape
    nlat, nlon = lax.axis_size("lat"), lax.axis_size("lon")
    ys, zn = nlat // X_LO, nlon // (2 * X_HI)
    lat, lon = lax.axis_index("lat"), lax.axis_index("lon")
    x_lo, y = lat // ys, lat % ys
    x_hi, z, core = lon // (2 * zn), (lon // 2) % zn, lon % 2
    x = x_hi * X_LO + x_lo
    me_q = x * ys + y
    nq = XS * ys
    blocks = rows // 8
    circle = nlon * L
    first_row, total_rows = lat * rows, rows * nlat
    is_top = lat == 0
    is_polar = is_top | (lat == nlat - 1)

    def place(xx, yy, zz, cc):
        return {"lat": (xx % X_LO) * ys + yy, "lon": (xx // X_LO) * (2 * zn) + zz * 2 + cc}

    def reach(o):
        dx, dy = o // ys, o % ys
        return min(dx, XS - dx) + min(dy, ys - dy)

    xy_order = sorted(range(1, nq), key=lambda o: -reach(o))

    near, mid = zn // 4, zn // 2

    def z_offset(i):
        return mid + (1 - 2 * (i % 2)) * ((i + 1) // 2)

    near_order = [d for n in range(near, 0, -1) for d in (n, zn - n)]

    def xy_peer(o):
        xx, yy = (x + o // ys) % XS, (y + o % ys) % ys
        return xx * ys + yy, place(xx, yy, z, core)

    def z_peer(d):
        zz = (z + d) % zn
        return zz, place(x, y, zz, core)

    def beside(dlat, dlon):
        return {"lat": (lat + dlat + nlat) % nlat, "lon": (lon + dlon + nlon) % nlon}

    partner = place(x, y, z, 1 - core)
    x_other = place((x + X_LO) % XS, y, z, core)

    def remote(src, dst, ss, rs, dev):
        return pltpu.make_async_remote_copy(
            src_ref=src, dst_ref=dst, send_sem=ss, recv_sem=rs, device_id=dev, device_id_type=MESH
        )

    def loop(lo, hi, f):
        def body(i, c):
            f(i)
            return c

        lax.fori_loop(lo, hi, body, 0)

    barrier = pltpu.get_barrier_semaphore()

    def greet(dev):
        pl.semaphore_signal(barrier, inc=1, device_id=dev, device_id_type=MESH)

    @pl.when(is_polar)
    def _():
        for d in near_order:
            greet(place((x + X_LO) % XS, y, (z + d) % zn, core))

    for d in near_order:
        greet(z_peer(d)[1])
    for o in xy_order:
        greet(xy_peer(o)[1])
    for dlat, dlon in ((1, 1), (1, -1), (-1, 1), (-1, -1), (0, 1), (0, -1)):
        greet(beside(dlat, dlon))

    loads = [
        pltpu.make_async_copy(a, b, load_sem.at[i])
        for i, (a, b) in enumerate((
            (band_hbm, band),
            (width_hbm, width),
            (cycle_hbm, circ),
            (sig, s_o.at[pl.ds(1, rows)]),
            (cot, c_o.at[pl.ds(1, rows)]),
            (w_hbm, w),
        ))
    ]
    for copy in loads:
        copy.start()
    slab_at = jnp.where(is_top, 0, rows - SLAB)
    pole_at = jnp.where(is_top, 0, rows - P_SIZE)
    sig_slab = sig.at[pl.ds(slab_at, SLAB)]
    cot_slab = cot.at[pl.ds(pole_at, P_SIZE)]
    sig_rows, cot_rows = pl.ds(0, SLAB), pl.ds(SLAB, P_SIZE)

    def seen(d):
        return mid - d if d <= mid else mid + zn - d

    def near_z(d):
        src = slab.at[:, x_hi, mid, core]
        dst = slab.at[:, x_hi, seen(d), core]
        return remote(src, dst, pc_ss.at[d], pc_rs.at[d], z_peer(d)[1])

    def cot_x(d):
        dst = slab.at[cot_rows, x_hi, seen(d), core]
        dev = place((x + X_LO) % XS, y, (z + d) % zn, core)
        src = slab.at[cot_rows, x_hi, mid, core]
        return remote(src, dst, px_ss.at[d], px_rs.at[d], dev)

    def cot_core():
        part = slab.at[cot_rows, :, pl.ds(mid - near, 2 * near + 1), core]
        return remote(part, part, pk_sem.at[0], pk_sem.at[1], partner)

    def far_copy(i):
        src, dst, n, d = (
            (mid - near, 0, near, near), (mid + 1, mid + near + 1, near - 1, zn - near)
        )[i]
        return remote(
            slab.at[:, x_hi, pl.ds(src, n), core], slab.at[:, x_hi, pl.ds(dst, n), core],
            ps_ss.at[i], ps_rs.at[i], z_peer(d)[1],
        )

    fars = [0, 1] if near > 1 else [0]
    spans = [(cot_rows, 0, mid - near), (cot_rows, mid + near + 1, mid - near - 1), (sig_rows, 0, zn)]
    spans = [span for span in spans if span[2] > 0]

    def rest_core(i):
        held, lo, n = spans[i]
        part = slab.at[held, x_hi, pl.ds(lo, n), core]
        return remote(part, part, pb_ss.at[i], pb_rs.at[i], partner)

    def part_copy():
        return remote(part_s, part_r, pp_sem.at[0], pp_sem.at[1], x_other)

    own_slab = [
        pltpu.make_async_copy(cot_slab, slab.at[cot_rows, x_hi, mid, core], own_sem.at[0]),
        pltpu.make_async_copy(sig_slab, slab.at[sig_rows, x_hi, mid, core], own_sem.at[1]),
    ]

    @pl.when(is_polar)
    def _():
        for copy in own_slab:
            copy.start()
        for copy in own_slab:
            copy.wait()

    greeted = 6 + (nq - 1) + 2 * near
    pl.semaphore_wait(barrier, jnp.where(is_polar, greeted + 2 * near, greeted))
    for i, d in enumerate((near, zn - near)):
        pl.semaphore_signal(far_sem.at[i], inc=1, device_id=z_peer(d)[1], device_id_type=MESH)

    @pl.when(is_polar)
    def _():
        for d in near_order:
            cot_x(d).start()
            near_z(d).start()
        cot_x(0).start()

    def halo_copies(src, own, left, right, n):
        last, first = src.at[pl.ds(rows - 1, 1)], src.at[pl.ds(0, 1)]
        top, bottom = pl.ds(0, 1), pl.ds(rows + 1, 1)
        spec = (
            (last, left.at[top], beside(1, 1)),
            (last, right.at[top], beside(1, -1)),
            (first, left.at[bottom], beside(-1, 1)),
            (first, right.at[bottom], beside(-1, -1)),
            (last, own.at[top], beside(1, 0)),
            (first, own.at[bottom], beside(-1, 0)),
            (src, left.at[pl.ds(1, rows)], beside(0, 1)),
            (src, right.at[pl.ds(1, rows)], beside(0, -1)),
        )
        return [
            remote(a, b, halo_ss.at[n + i], halo_rs.at[n + i], dev)
            for i, (a, b, dev) in enumerate(spec)
        ]

    sig_halo = halo_copies(sig, s_o, s_l, s_r, 0)
    cot_halo = halo_copies(cot, c_o, c_l, c_r, 8)
    for copy in sig_halo:
        copy.start()

    loads[0].wait()
    loads[1].wait()
    lanes = 256
    taps = range(2 * R + 1)
    lags = 2 * H + 1
    used = (2 * R + 1) * lags * K
    taps_v[...] = jnp.zeros_like(taps_v)
    for r in taps:
        for d in range(lags):
            taps_v[pl.ds((r * lags + d) * K, K), :] = band[r, d].astype(F32)
    taps_t[pl.ds(0, 16), :] = jnp.zeros((16, lanes), BF16)
    taps_t[pl.ds(16, total_rows), :] = jnp.transpose(taps_v[...])[:total_rows].astype(BF16)
    taps_t[pl.ds(16 + total_rows, 16), :] = jnp.zeros((16, lanes), BF16)
    mine = taps_t[pl.ds(pl.multiple_of(first_row, 16), rows + 32), :]
    held = lax.broadcasted_iota(jnp.int32, (lanes, 1), 0)
    held_k, held_r, held_d = held % K, held // (K * lags), held // K % lags
    lane = lax.broadcasted_iota(jnp.int32, (lanes, lanes), 1)
    to_f = jnp.where(held < used, held_r * 3 * L + 2 * H - held_d, -1)
    to_b = jnp.where(held < used, (2 * R - held_r) * 3 * L + held_d, -1)
    for k in range(K):
        placed = [
            dot(mine, (lane == jnp.where(held_k == k, to, -1)).astype(F32).astype(BF16))
            for to in (to_f, to_b)
        ]
        bf[k] = placed[0][16 : 16 + rows]
        slots = lax.broadcasted_iota(jnp.int32, (1, lanes), 1) // (3 * L)
        above, same, below = (placed[1][15 + s : 15 + s + rows] for s in taps)
        bb[k] = jnp.where(slots == 0, above, jnp.where(slots == 1, same, below))
    lane_row = lax.broadcasted_iota(jnp.int32, (1, lanes), 1)
    slot = lane_row // (3 * L)
    away = jnp.abs(lane_row - slot * (3 * L) - H)

    def width_of(i):
        row = first_row + i
        held = width[(row + total_rows) % total_rows]
        return jnp.where((row >= P_SIZE) & (row < total_rows - P_SIZE), held, -1)

    def build(src, dst, backward):
        def block(b):
            allowed = []
            for i in range(8):
                row = b * 8 + i
                if backward:
                    near = [width_of(row + s - R) for s in taps]
                    limit = jnp.where(slot == 0, near[0], jnp.where(slot == 1, near[1], near[2]))
                else:
                    limit = width_of(row)
                allowed.append(away <= limit)
            for k in range(K):
                tile = src[k, pl.ds(pl.multiple_of(b * 8, 8), 8), :]
                for i in range(0, 8, 2):
                    parts = [
                        pltpu.roll(
                            jnp.broadcast_to(jnp.where(allowed[j], tile[j : j + 1], 0.0), (L, lanes)),
                            j * 3 * L, 1, stride=1, stride_axis=0,
                        )
                        for j in (i, i + 1)
                    ]
                    dst[b, pl.ds((k * 8 + i) * L, 2 * L), :] = jnp.concatenate(parts, 0).astype(BF16)

        loop(0, blocks, block)

    def window(o, left, right, b):
        at = pl.ds(b * 8, 10)
        parts = [ref[at].astype(F32) for ref in (left, o, right)]
        both = jnp.concatenate(parts, 1).reshape(30 * L, chans)
        return jnp.concatenate([both, jnp.zeros((2 * L, chans), F32)], 0).astype(BF16)

    build(bf, amat, False)

    loads[2].wait()

    def cycle_rows(src, r):
        row = jnp.broadcast_to(src[r : r + 1, :], (L, circle))
        return pltpu.roll(row, 0, 1, stride=1, stride_axis=0)

    @pl.when(is_polar)
    def _():
        none = jnp.zeros((1, circle), F32)
        for k in range(K):
            for p in range(P_SIZE):

                def tap(r):
                    if not 0 <= r <= 2 * R:
                        return none
                    held = circ[k, r].astype(F32)
                    return jnp.where(is_top, held[p : p + 1], held[P_SIZE + p : P_SIZE + p + 1])

                for r in taps:
                    at = (k * SLAB + r) * P_SIZE + p
                    cyc[at : at + 1, :] = jnp.where(is_top, tap(r - p + R), tap(r - p))
        col = lax.broadcasted_iota(jnp.int32, (1, circle), 1)
        t, c = col // (8 * L) - near, col % (8 * L)
        xh, o, cc, l = c // (4 * L), c // (2 * L) % 2, c // L % 2, c % L
        z_cot, z_sig = (z + t + o + zn) % zn, (z - t + zn) % zn
        lag = (xh - x_hi) * (circle // 2) + (z_cot - z_sig) * (2 * L) + (cc - core) * L + l
        lag = (lag + 2 * circle) % circle
        pick = (lax.broadcasted_iota(jnp.int32, (circle, circle), 0) == lag).astype(F32).astype(BF16)
        for p in range(P_SIZE):
            turned = [cycle_rows(cyc, n * P_SIZE + p) for n in range(K * SLAB)]
            qt[p] = dot(jnp.concatenate(turned, 0).astype(BF16), pick).astype(BF16)
        for d in [0] + near_order:
            cot_x(d).wait_recv()
        for d in near_order:
            near_z(d).wait_recv()
        cot_core().start()

    loads[3].wait()
    for copy in sig_halo:
        copy.wait_recv()
    for copy in cot_halo:
        copy.start()

    @pl.when(is_polar)
    def _():
        for i in fars:
            far_copy(i).start()

    def forward(b):
        part = dot(amat[b], window(s_o, s_l, s_r, b)).astype(BF16)
        for k in range(K):
            filt[k, pl.ds(b * 64, 64), :] = part[k * 64 : (k + 1) * 64]

    loop(0, blocks, forward)
    loads[4].wait()

    def fold(b):
        cot2[pl.ds(b * 64, 64), :] = (
            c_o[pl.ds(1 + b * 8, 8)].astype(F32).reshape(64, chans).astype(BF16)
        )

    loop(0, blocks, fold)

    def cells(ref):
        held = ref.astype(F32)
        return held.reshape(-1, chans)

    @pl.when(is_polar)
    def _():
        cot_core().wait_recv()
        for i in range(2 * near):
            t = i - near
            turned = sum(
                dot(
                    qt[p, :, i * 8 * L : (i + 1) * 8 * L],
                    cells(slab[SLAB + p, :, mid + t : mid + t + 2]).astype(BF16),
                )
                for p in range(P_SIZE)
            )
            for k in range(K):
                gw[k, pl.ds(i * SLAB * L, SLAB * L), :] = turned[k * SLAB * L : (k + 1) * SLAB * L]
            sw[pl.ds(i * SLAB * L, SLAB * L), :] = cells(slab[0:SLAB, x_hi, mid - t, core])
    half_rows = K * chans // 2

    def weight_half(c):
        for i in range(K // 2):
            k = c * (K // 2) + i
            wall[pl.ds(i * chans, chans), :] = lax.dot_general(
                filt[k], cot2[...], (((0,), (0,)), ((), ())), preferred_element_type=F32
            )

        @pl.when(is_polar)
        def _():
            for i in range(K // 2):
                wall[pl.ds(i * chans, chans), :] += lax.dot_general(
                    sw[...].astype(BF16), gw[c * (K // 2) + i].astype(BF16),
                    (((0,), (0,)), ((), ())), preferred_element_type=F32,
                )

    weight_half(1 - core)
    wsend[...] = wall[...].astype(BF16)
    to_core = remote(wsend, wrecv, core_sem.at[0], core_sem.at[1], partner)
    to_core.start()
    weight_half(core)
    piece = half_rows // nq
    to_core.wait_recv()
    summed = wall[...] + wrecv[...].astype(F32)
    half[...] = summed.reshape(nq, piece, chans)
    xs[...] = summed.astype(BF16).reshape(nq, piece, chans)

    def xy_copy(o):
        q, dev = xy_peer(o)
        return remote(xs.at[q], xr.at[o], x_ss.at[o], x_rs.at[o], dev)

    for o in xy_order:
        xy_copy(o).start()

    for i in range(2):
        pl.semaphore_wait(far_sem.at[i], 1)

    loads[5].wait()
    chunk = 8

    def mix_out(b):
        at = pl.ds(b * chunk * L, chunk * L)
        acc = sum(dot(filt[k, at, :], w[k]) for k in range(K))
        conv_v[pl.ds(b * chunk, chunk)] = acc.reshape(chunk, L, chans).astype(BF16)

    loop(0, rows // chunk, mix_out)
    build(bb, bmat, True)
    for copy in cot_halo:
        copy.wait_recv()

    def backward(b):
        part = dot(bmat[b], window(c_o, c_l, c_r, b))
        for k in range(K):
            grad[k, pl.ds(b * 64, 64), :] = part[k * 64 : (k + 1) * 64]

    loop(0, blocks, backward)

    @pl.when(is_polar)
    def _():
        start = cyc[...]
        from_lag = lax.broadcasted_iota(jnp.int32, (circle, circle), 0)
        to_lag = lax.broadcasted_iota(jnp.int32, (circle, circle), 1)
        turned = ((from_lag + to_lag) % circle == 0).astype(F32).astype(BF16)
        rev[...] = pltpu.roll(dot(start.astype(BF16), turned), lon * L, 1)
        cyc[...] = pltpu.roll(start, lon * L, 1)
        side = circle // 2
        shift = (side + (mid - z) * 2 * L) % side

        def circulant(src, rows_of, dst, at):
            full = jnp.concatenate([cycle_rows(src, n) for n in rows_of], 0)
            for h in range(2):
                turned_side = pltpu.roll(full[:, h * side : (h + 1) * side], shift, 1)
                dst[h, :, pl.ds(at, side)] = turned_side.astype(BF16)

        for p in range(P_SIZE):
            circulant(cyc, [n * P_SIZE + p for n in range(K * SLAB)], qb, p * side)
        for r in taps:
            circulant(
                rev, [(k * SLAB + r) * P_SIZE + p for k in range(K) for p in range(P_SIZE)], qf, r * side
            )

    loop(1, nq, lambda o: xy_copy(o).wait_recv())
    total = half[me_q]
    for o in range(1, nq):
        total = total + xr[o].astype(F32)

    for p in range(4):
        zs[p] = total[
            (p // 2) * (piece // 2) : (p // 2 + 1) * (piece // 2), (p % 2) * 128 : (p % 2 + 1) * 128
        ].astype(BF16)

    def z_copy(d):
        zz, dev = z_peer(d)
        return remote(zs.at[zz % 4], zr.at[z], z_ss.at[d], z_rs.at[d], dev)

    loop(0, zn - 1, lambda i: z_copy(z_offset(i)).start())
    zr[z] = zs[z % 4]

    @pl.when(is_polar)
    def _():
        for i in fars:
            far_copy(i).wait_recv()
        for i in range(len(spans)):
            rest_core(i).start()

    @pl.when(is_polar)
    def _():
        for i in range(len(spans)):
            rest_core(i).wait_recv()
        side = circle // 2
        held_rows = [cells(slab[r, x_hi]).astype(BF16) for r in range(SLAB + P_SIZE)]

        def share(h):
            front = sum(dot(qf[h, :, r * side : (r + 1) * side], held_rows[r]) for r in range(SLAB))
            back = sum(
                dot(qb[h, :, p * side : (p + 1) * side], held_rows[SLAB + p]) for p in range(P_SIZE)
            )
            return jnp.concatenate([front, back], 0)

        part_s[...] = share(1 - x_hi).astype(BF16)
        part_copy().start()
        own_part[...] = share(x_hi)

    loop(0, zn - 1, lambda i: z_copy(z_offset(i)).wait_recv())
    acc = zr[0].astype(F32)
    for s in range(1, zn):
        acc = acc + zr[s].astype(F32)
    za[z % 4] = (acc * F32(1.0 / math.sqrt(total_rows * circle))).astype(BF16)
    hand = (2, 1, zn - 1)

    def za_copy(i):
        dst = za.at[z % 4]
        return remote(dst, dst, za_ss.at[i], za_rs.at[i], z_peer(hand[i])[1])

    for i in range(3):
        za_copy(i).start()

    for i in range(3):
        za_copy(i).wait_recv()
    lines = [jnp.concatenate([za[2 * i].astype(F32), za[2 * i + 1].astype(F32)], 1) for i in range(2)]
    fin[core, me_q] = jnp.concatenate(lines, 0).astype(BF16)

    def xa_copy(o):
        dst = fin.at[core, me_q]
        return remote(dst, dst, xa_ss.at[o], xa_rs.at[o], xy_peer(o)[1])

    for o in xy_order:
        xa_copy(o).start()

    def mix_back(b):
        at = pl.ds(b * chunk * L, chunk * L)
        acc = sum(
            lax.dot_general(
                grad[k, at, :].astype(BF16), w[k], (((1,), (1,)), ((), ())),
                preferred_element_type=F32,
            )
            for k in range(K)
        )
        sg_v[pl.ds(b * chunk, chunk)] = acc.reshape(chunk, L, chans).astype(BF16)

    loop(0, rows // chunk, mix_back)

    @pl.when(is_polar)
    def _():
        part_copy().wait_recv()
        sums = own_part[...] + part_r[...].astype(F32)
        front, extra = sums[: K * P_SIZE * L], sums[K * P_SIZE * L :]
        out = sum(dot(front[k * 16 : (k + 1) * 16].astype(BF16), w[k]) for k in range(K))
        conv_v[pl.ds(pole_at, P_SIZE)] = out.reshape(P_SIZE, L, chans).astype(BF16)
        at = pl.multiple_of(slab_at * L, 8)
        back = sum(
            lax.dot_general(
                (grad[k, pl.ds(at, SLAB * L), :] + extra[k * SLAB * L : (k + 1) * SLAB * L]).astype(BF16),
                w[k], (((1,), (1,)), ((), ())), preferred_element_type=F32,
            )
            for k in range(K)
        )
        sg_v[pl.ds(slab_at, SLAB)] = back.reshape(SLAB, L, chans).astype(BF16)

    sg_copy = pltpu.make_async_copy(sg_v, sgrad_out, out_sem.at[1])
    sg_copy.start()
    conv_copy = pltpu.make_async_copy(conv_v, conv_out, out_sem.at[0])
    conv_copy.start()

    def column(c, dx):
        return fin.at[c, pl.ds((x - dx + XS) % XS * ys, ys)]

    def swap(i, dx):
        part = column(core, dx)
        return remote(part, part, fc_ss.at[i], fc_rs.at[i], partner)

    def leave(i, c, dx):
        dst = wgrad_out.at[c, pl.ds((x - dx + XS) % XS * ys, ys)]
        return pltpu.make_async_copy(column(c, dx), dst, out_sem.at[i])

    columns = list(enumerate((0, 1, XS - 1, 2)))
    for i, dx in columns:
        for o in range(dx * ys, (dx + 1) * ys):
            if o > 0:
                xa_copy(o).wait_recv()
        swap(i, dx).start()
        leave(2 + i, core, dx).start()

    @pl.when(is_polar)
    def _():
        for d in near_order:
            near_z(d).wait_send()
        for d in [0] + near_order:
            cot_x(d).wait_send()
        cot_core().wait_send()
        for i in fars:
            far_copy(i).wait_send()
        for i in range(len(spans)):
            rest_core(i).wait_send()
        part_copy().wait_send()

    for copy in sig_halo + cot_halo:
        copy.wait_send()
    to_core.wait_send()
    loop(1, nq, lambda o: xy_copy(o).wait_send())
    loop(1, zn, lambda d: z_copy(d).wait_send())
    for i in range(3):
        za_copy(i).wait_send()
    loop(1, nq, lambda o: xa_copy(o).wait_send())
    conv_copy.wait()
    sg_copy.wait()
    for i, dx in columns:
        swap(i, dx).wait()
        leave(2 + XS + i, 1 - core, dx).start()
    for i, dx in columns:
        leave(2 + i, core, dx).wait()
        leave(2 + XS + i, 1 - core, dx).wait()


def finish(conv, sgrad, wgrad):
    parts = 4

    def body(conv_in, sg_in, wg_in, conv_out, sg_out, wg_out, held, wide, fields, sems):
        ends = [(conv_in, fields.at[0], conv_out), (sg_in, fields.at[1], sg_out)]
        ends += [(wg_in.at[k], held.at[k], wg_out.at[k]) for k in range(parts)]
        loads = [pltpu.make_async_copy(a, b, sems.at[0, i]) for i, (a, b, _) in enumerate(ends)]
        stores = [
            pltpu.make_async_copy(b if i < 2 else wide.at[i - 2], c, sems.at[1, i])
            for i, (_, b, c) in enumerate(ends)
        ]
        for copy in loads:
            copy.start()
        for i in range(2 + parts):
            loads[i].wait()
            if i >= 2:
                wide[i - 2] = held[i - 2].astype(F32)
            stores[i].start()
        for copy in stores:
            copy.wait()

    return pl.pallas_call(
        body,
        out_shape=(
            jax.ShapeDtypeStruct(conv.shape, conv.dtype),
            jax.ShapeDtypeStruct(sgrad.shape, sgrad.dtype),
            jax.ShapeDtypeStruct(wgrad.shape, F32),
        ),
        in_specs=[pl.BlockSpec(memory_space=pl.ANY)] * 3,
        out_specs=[pl.BlockSpec(memory_space=pl.ANY)] * 3,
        scratch_shapes=[
            pltpu.VMEM(wgrad.shape, BF16), pltpu.VMEM(wgrad.shape, F32),
            pltpu.VMEM((2,) + conv.shape, BF16), pltpu.SemaphoreType.DMA((2, 2 + parts)),
        ],
        compiler_params=pltpu.CompilerParams(vmem_limit_bytes=60 * 2**20),
    )(conv, sgrad, wgrad)


def local(signal, cotangent, weights, band_kernel, cycle_kernel, support_width):
    rows, _, chans = signal.shape
    nlat, nlon = lax.axis_size("lat"), lax.axis_size("lon")
    ys, zn = nlat // X_LO, nlon // (2 * X_HI)
    nq = XS * ys
    circle = nlon * L
    blocks, cells = rows // 8, rows * L
    half_rows = K * chans // 2
    piece = half_rows // nq
    band = band_kernel.transpose(2, 3, 0, 1)
    cycle = cycle_kernel.transpose(0, 2, 1, 3)
    dma = pltpu.SemaphoreType.DMA
    ext = (rows + 2, L, chans)
    base = pltpu.VMEM((K, rows, 256), F32)
    turns = pltpu.VMEM((K * SLAB * P_SIZE, circle), F32)
    matrices = pltpu.VMEM((blocks, K * 64, 256), BF16)
    scratch = (
        [pltpu.VMEM(ext, BF16)] * 6
        + [pltpu.VMEM(weights.shape, BF16)]
        + [pltpu.VMEM(band.shape, BF16)]
        + [pltpu.VMEM((K, 2 * R + 1, 2 * P_SIZE, circle), BF16)]
        + [pltpu.SMEM(support_width.shape, jnp.int32)]
        + [pltpu.VMEM((256, rows * nlat), F32), pltpu.VMEM((rows * nlat + 32, 256), BF16)]
        + [base] * 2 + [turns] * 2 + [matrices] * 2
        + [pltpu.VMEM((K, cells, chans), BF16), pltpu.VMEM((K, cells, chans), F32)]
        + [pltpu.VMEM((cells, chans), BF16)]
        + [pltpu.VMEM((rows, L, chans), BF16)] * 2
        + [pltpu.VMEM((SLAB + P_SIZE, X_HI, zn, 2, L, chans), BF16)]
        + [pltpu.VMEM((2, K * P_SIZE * L, SLAB * circle // 2), BF16)]
        + [pltpu.VMEM((2, K * SLAB * L, P_SIZE * circle // 2), BF16)]
        + [pltpu.VMEM((P_SIZE, K * SLAB * L, circle), BF16)]
        + [pltpu.VMEM((K, zn // 2 * SLAB * L, chans), F32), pltpu.VMEM((zn // 2 * SLAB * L, chans), F32)]
        + [pltpu.VMEM((K * (P_SIZE + SLAB) * L, chans), BF16)] * 2
        + [pltpu.VMEM((K * (P_SIZE + SLAB) * L, chans), F32)]
        + [pltpu.VMEM((half_rows, chans), F32)]
        + [pltpu.VMEM((half_rows, chans), BF16)] * 2
        + [pltpu.VMEM((nq, piece, chans), F32)]
        + [pltpu.VMEM((nq, piece, chans), BF16)] * 2
        + [pltpu.VMEM((n, piece // 2, 128), BF16) for n in (4, zn, 4)]
        + [pltpu.VMEM((2, nq, piece, chans), BF16)]
        + [pltpu.SemaphoreType.REGULAR((2,))]
        + [dma((n,)) for n in (
            6, 16, 16, 2, zn, zn, zn, zn, 2,
            2, 2, 3, 3, 2,
            2, nq, nq, zn, zn, 3, 3, nq, nq, XS, XS, 2 + 2 * XS,
        )]
    )
    field = jax.ShapeDtypeStruct(signal.shape, BF16)
    conv, sgrad, wgrad = pl.pallas_call(
        kernel,
        out_shape=(field, field, jax.ShapeDtypeStruct((2, nq, piece, chans), BF16)),
        in_specs=[pl.BlockSpec(memory_space=pl.ANY)] * 6,
        out_specs=[pl.BlockSpec(memory_space=pl.ANY)] * 3,
        scratch_shapes=scratch,
        compiler_params=pltpu.CompilerParams(
            collective_id=0, has_side_effects=True, vmem_limit_bytes=60 * 2**20
        ),
        cost_estimate=pl.CostEstimate(flops=10**9, bytes_accessed=4 * 10**6, transcendentals=0),
    )(signal, cotangent, weights, band, cycle, support_width)
    return finish(conv, sgrad, wgrad.reshape(K, chans, chans))


def solution(mesh):
    placed = (P("lat", "lon", None), P("lat", "lon", None), P(), P(), P(), P())
    return jax.shard_map(
        local,
        mesh=mesh,
        in_specs=placed,
        out_specs=(P("lat", "lon", None), P("lat", "lon", None), P()),
        check_vma=False,
    )
```

```python
import functools
import math

import jax
import jax.numpy as jnp
from jax import lax
from jax.experimental import pallas as pl
from jax.experimental.pallas import tpu as pltpu
from jax.sharding import PartitionSpec as P

K = 4
R = 1
H = 8
P_SIZE = 2
L = 8
SLAB = P_SIZE + R
X_HI = 2
X_LO = 2
XS = X_HI * X_LO
MESH = pl.DeviceIdType.MESH
F32 = jnp.float32
BF16 = jnp.bfloat16


def dot(a, b):
    return jnp.dot(a, b, preferred_element_type=F32)


def kernel(
    sig, cot, w_hbm, band_hbm, cycle_hbm, width_hbm,
    conv_out, sgrad_out, wgrad_out,
    s_o, s_l, s_r, c_o, c_l, c_r, w, band, circ, width, taps_v, taps_t,
    bf, bb, cyc, rev, amat, bmat, filt, grad, cot2, conv_v, sg_v,
    slab, qf, qb, qt, gw, sw, part_s, part_r, own_part,
    wall, wsend, wrecv, half, xs, xr, zs, zr, za, fin,
    far_sem, load_sem, halo_ss, halo_rs, own_sem, pc_ss, pc_rs, px_ss, px_rs, pk_sem,
    ps_ss, ps_rs, pb_ss, pb_rs, pp_sem,
    core_sem, x_ss, x_rs, z_ss, z_rs, za_ss, za_rs, xa_ss, xa_rs, fc_ss, fc_rs, out_sem,
):
    rows, _, chans = sig.shape
    nlat, nlon = lax.axis_size("lat"), lax.axis_size("lon")
    ys, zn = nlat // X_LO, nlon // (2 * X_HI)
    lat, lon = lax.axis_index("lat"), lax.axis_index("lon")
    x_lo, y = lat // ys, lat % ys
    x_hi, z, core = lon // (2 * zn), (lon // 2) % zn, lon % 2
    x = x_hi * X_LO + x_lo
    me_q = x * ys + y
    nq = XS * ys
    blocks = rows // 8
    circle = nlon * L
    first_row, total_rows = lat * rows, rows * nlat
    is_top = lat == 0
    is_polar = is_top | (lat == nlat - 1)

    def place(xx, yy, zz, cc):
        return {"lat": (xx % X_LO) * ys + yy, "lon": (xx // X_LO) * (2 * zn) + zz * 2 + cc}

    def reach(o):
        dx, dy = o // ys, o % ys
        return min(dx, XS - dx) + min(dy, ys - dy)

    xy_order = sorted(range(1, nq), key=lambda o: -reach(o))

    near, mid = zn // 4, zn // 2

    def z_offset(i):
        return mid + (1 - 2 * (i % 2)) * ((i + 1) // 2)

    near_order = [d for n in range(near, 0, -1) for d in (n, zn - n)]

    def xy_peer(o):
        xx, yy = (x + o // ys) % XS, (y + o % ys) % ys
        return xx * ys + yy, place(xx, yy, z, core)

    def z_peer(d):
        zz = (z + d) % zn
        return zz, place(x, y, zz, core)

    def beside(dlat, dlon):
        return {"lat": (lat + dlat + nlat) % nlat, "lon": (lon + dlon + nlon) % nlon}

    partner = place(x, y, z, 1 - core)
    x_other = place((x + X_LO) % XS, y, z, core)

    def remote(src, dst, ss, rs, dev):
        return pltpu.make_async_remote_copy(
            src_ref=src, dst_ref=dst, send_sem=ss, recv_sem=rs, device_id=dev, device_id_type=MESH
        )

    def loop(lo, hi, f):
        def body(i, c):
            f(i)
            return c

        lax.fori_loop(lo, hi, body, 0)

    barrier = pltpu.get_barrier_semaphore()

    def greet(dev):
        pl.semaphore_signal(barrier, inc=1, device_id=dev, device_id_type=MESH)

    @pl.when(is_polar)
    def _():
        for d in near_order:
            greet(place((x + X_LO) % XS, y, (z + d) % zn, core))

    for d in near_order:
        greet(z_peer(d)[1])
    for o in xy_order:
        greet(xy_peer(o)[1])
    for dlat, dlon in ((1, 1), (1, -1), (-1, 1), (-1, -1), (0, 1), (0, -1)):
        greet(beside(dlat, dlon))

    loads = [
        pltpu.make_async_copy(a, b, load_sem.at[i])
        for i, (a, b) in enumerate((
            (band_hbm, band),
            (width_hbm, width),
            (cycle_hbm, circ),
            (sig, s_o.at[pl.ds(1, rows)]),
            (cot, c_o.at[pl.ds(1, rows)]),
            (w_hbm, w),
        ))
    ]
    for copy in loads:
        copy.start()
    slab_at = jnp.where(is_top, 0, rows - SLAB)
    pole_at = jnp.where(is_top, 0, rows - P_SIZE)
    sig_slab = sig.at[pl.ds(slab_at, SLAB)]
    cot_slab = cot.at[pl.ds(pole_at, P_SIZE)]
    sig_rows, cot_rows = pl.ds(0, SLAB), pl.ds(SLAB, P_SIZE)

    def seen(d):
        return mid - d if d <= mid else mid + zn - d

    def near_z(d):
        src = slab.at[:, x_hi, mid, core]
        dst = slab.at[:, x_hi, seen(d), core]
        return remote(src, dst, pc_ss.at[d], pc_rs.at[d], z_peer(d)[1])

    def cot_x(d):
        dst = slab.at[cot_rows, x_hi, seen(d), core]
        dev = place((x + X_LO) % XS, y, (z + d) % zn, core)
        src = slab.at[cot_rows, x_hi, mid, core]
        return remote(src, dst, px_ss.at[d], px_rs.at[d], dev)

    def cot_core():
        part = slab.at[cot_rows, :, pl.ds(mid - near, 2 * near + 1), core]
        return remote(part, part, pk_sem.at[0], pk_sem.at[1], partner)

    def far_copy(i):
        src, dst, n, d = (
            (mid - near, 0, near, near), (mid + 1, mid + near + 1, near - 1, zn - near)
        )[i]
        return remote(
            slab.at[:, x_hi, pl.ds(src, n), core], slab.at[:, x_hi, pl.ds(dst, n), core],
            ps_ss.at[i], ps_rs.at[i], z_peer(d)[1],
        )

    fars = [0, 1] if near > 1 else [0]
    spans = [(cot_rows, 0, mid - near), (cot_rows, mid + near + 1, mid - near - 1), (sig_rows, 0, zn)]
    spans = [span for span in spans if span[2] > 0]

    def rest_core(i):
        held, lo, n = spans[i]
        part = slab.at[held, x_hi, pl.ds(lo, n), core]
        return remote(part, part, pb_ss.at[i], pb_rs.at[i], partner)

    def part_copy():
        return remote(part_s, part_r, pp_sem.at[0], pp_sem.at[1], x_other)

    own_slab = [
        pltpu.make_async_copy(cot_slab, slab.at[cot_rows, x_hi, mid, core], own_sem.at[0]),
        pltpu.make_async_copy(sig_slab, slab.at[sig_rows, x_hi, mid, core], own_sem.at[1]),
    ]

    @pl.when(is_polar)
    def _():
        for copy in own_slab:
            copy.start()
        for copy in own_slab:
            copy.wait()

    greeted = 6 + (nq - 1) + 2 * near
    pl.semaphore_wait(barrier, jnp.where(is_polar, greeted + 2 * near, greeted))
    for i, d in enumerate((near, zn - near)):
        pl.semaphore_signal(far_sem.at[i], inc=1, device_id=z_peer(d)[1], device_id_type=MESH)

    @pl.when(is_polar)
    def _():
        for d in near_order:
            cot_x(d).start()
            near_z(d).start()
        cot_x(0).start()

    def halo_copies(src, own, left, right, n):
        last, first = src.at[pl.ds(rows - 1, 1)], src.at[pl.ds(0, 1)]
        top, bottom = pl.ds(0, 1), pl.ds(rows + 1, 1)
        spec = (
            (last, left.at[top], beside(1, 1)),
            (last, right.at[top], beside(1, -1)),
            (first, left.at[bottom], beside(-1, 1)),
            (first, right.at[bottom], beside(-1, -1)),
            (last, own.at[top], beside(1, 0)),
            (first, own.at[bottom], beside(-1, 0)),
            (src, left.at[pl.ds(1, rows)], beside(0, 1)),
            (src, right.at[pl.ds(1, rows)], beside(0, -1)),
        )
        return [
            remote(a, b, halo_ss.at[n + i], halo_rs.at[n + i], dev)
            for i, (a, b, dev) in enumerate(spec)
        ]

    sig_halo = halo_copies(sig, s_o, s_l, s_r, 0)
    cot_halo = halo_copies(cot, c_o, c_l, c_r, 8)
    for copy in sig_halo:
        copy.start()

    loads[0].wait()
    loads[1].wait()
    lanes = 256
    taps = range(2 * R + 1)
    lags = 2 * H + 1
    used = (2 * R + 1) * lags * K
    taps_v[...] = jnp.zeros_like(taps_v)
    for r in taps:
        for d in range(lags):
            taps_v[pl.ds((r * lags + d) * K, K), :] = band[r, d].astype(F32)
    taps_t[pl.ds(0, 16), :] = jnp.zeros((16, lanes), BF16)
    taps_t[pl.ds(16, total_rows), :] = jnp.transpose(taps_v[...])[:total_rows].astype(BF16)
    taps_t[pl.ds(16 + total_rows, 16), :] = jnp.zeros((16, lanes), BF16)
    mine = taps_t[pl.ds(pl.multiple_of(first_row, 16), rows + 32), :]
    held = lax.broadcasted_iota(jnp.int32, (lanes, 1), 0)
    held_k, held_r, held_d = held % K, held // (K * lags), held // K % lags
    lane = lax.broadcasted_iota(jnp.int32, (lanes, lanes), 1)
    to_f = jnp.where(held < used, held_r * 3 * L + 2 * H - held_d, -1)
    to_b = jnp.where(held < used, (2 * R - held_r) * 3 * L + held_d, -1)
    for k in range(K):
        placed = [
            dot(mine, (lane == jnp.where(held_k == k, to, -1)).astype(F32).astype(BF16))
            for to in (to_f, to_b)
        ]
        bf[k] = placed[0][16 : 16 + rows]
        slots = lax.broadcasted_iota(jnp.int32, (1, lanes), 1) // (3 * L)
        above, same, below = (placed[1][15 + s : 15 + s + rows] for s in taps)
        bb[k] = jnp.where(slots == 0, above, jnp.where(slots == 1, same, below))
    lane_row = lax.broadcasted_iota(jnp.int32, (1, lanes), 1)
    slot = lane_row // (3 * L)
    away = jnp.abs(lane_row - slot * (3 * L) - H)

    def width_of(i):
        row = first_row + i
        held = width[(row + total_rows) % total_rows]
        return jnp.where((row >= P_SIZE) & (row < total_rows - P_SIZE), held, -1)

    def build(src, dst, backward):
        def block(b):
            allowed = []
            for i in range(8):
                row = b * 8 + i
                if backward:
                    near = [width_of(row + s - R) for s in taps]
                    limit = jnp.where(slot == 0, near[0], jnp.where(slot == 1, near[1], near[2]))
                else:
                    limit = width_of(row)
                allowed.append(away <= limit)
            for k in range(K):
                tile = src[k, pl.ds(pl.multiple_of(b * 8, 8), 8), :]
                for i in range(0, 8, 2):
                    parts = [
                        pltpu.roll(
                            jnp.broadcast_to(jnp.where(allowed[j], tile[j : j + 1], 0.0), (L, lanes)),
                            j * 3 * L, 1, stride=1, stride_axis=0,
                        )
                        for j in (i, i + 1)
                    ]
                    dst[b, pl.ds((k * 8 + i) * L, 2 * L), :] = jnp.concatenate(parts, 0).astype(BF16)

        loop(0, blocks, block)

    def window(o, left, right, b):
        at = pl.ds(b * 8, 10)
        parts = [ref[at].astype(F32) for ref in (left, o, right)]
        both = jnp.concatenate(parts, 1).reshape(30 * L, chans)
        return jnp.concatenate([both, jnp.zeros((2 * L, chans), F32)], 0).astype(BF16)

    build(bf, amat, False)

    loads[2].wait()

    def cycle_rows(src, r):
        row = jnp.broadcast_to(src[r : r + 1, :], (L, circle))
        return pltpu.roll(row, 0, 1, stride=1, stride_axis=0)

    @pl.when(is_polar)
    def _():
        none = jnp.zeros((1, circle), F32)
        for k in range(K):
            for p in range(P_SIZE):

                def tap(r):
                    if not 0 <= r <= 2 * R:
                        return none
                    held = circ[k, r].astype(F32)
                    return jnp.where(is_top, held[p : p + 1], held[P_SIZE + p : P_SIZE + p + 1])

                for r in taps:
                    at = (k * SLAB + r) * P_SIZE + p
                    cyc[at : at + 1, :] = jnp.where(is_top, tap(r - p + R), tap(r - p))
        col = lax.broadcasted_iota(jnp.int32, (1, circle), 1)
        t, c = col // (8 * L) - near, col % (8 * L)
        xh, o, cc, l = c // (4 * L), c // (2 * L) % 2, c // L % 2, c % L
        z_cot, z_sig = (z + t + o + zn) % zn, (z - t + zn) % zn
        lag = (xh - x_hi) * (circle // 2) + (z_cot - z_sig) * (2 * L) + (cc - core) * L + l
        lag = (lag + 2 * circle) % circle
        pick = (lax.broadcasted_iota(jnp.int32, (circle, circle), 0) == lag).astype(F32).astype(BF16)
        for p in range(P_SIZE):
            turned = [cycle_rows(cyc, n * P_SIZE + p) for n in range(K * SLAB)]
            qt[p] = dot(jnp.concatenate(turned, 0).astype(BF16), pick).astype(BF16)
        for d in [0] + near_order:
            cot_x(d).wait_recv()
        for d in near_order:
            near_z(d).wait_recv()
        cot_core().start()

    loads[3].wait()
    for copy in sig_halo:
        copy.wait_recv()
    @pl.when(is_polar)
    def _():
        for i in fars:
            far_copy(i).start()

    def forward(b):
        part = dot(amat[b], window(s_o, s_l, s_r, b)).astype(BF16)
        for k in range(K):
            filt[k, pl.ds(b * 64, 64), :] = part[k * 64 : (k + 1) * 64]

    loop(0, blocks, forward)
    loads[4].wait()

    def fold(b):
        cot2[pl.ds(b * 64, 64), :] = (
            c_o[pl.ds(1 + b * 8, 8)].astype(F32).reshape(64, chans).astype(BF16)
        )

    loop(0, blocks, fold)

    def cells(ref):
        held = ref.astype(F32)
        return held.reshape(-1, chans)

    @pl.when(is_polar)
    def _():
        cot_core().wait_recv()
        for i in range(2 * near):
            t = i - near
            turned = sum(
                dot(
                    qt[p, :, i * 8 * L : (i + 1) * 8 * L],
                    cells(slab[SLAB + p, :, mid + t : mid + t + 2]).astype(BF16),
                )
                for p in range(P_SIZE)
            )
            for k in range(K):
                gw[k, pl.ds(i * SLAB * L, SLAB * L), :] = turned[k * SLAB * L : (k + 1) * SLAB * L]
            sw[pl.ds(i * SLAB * L, SLAB * L), :] = cells(slab[0:SLAB, x_hi, mid - t, core])
    half_rows = K * chans // 2

    def weight_half(c):
        for i in range(K // 2):
            k = c * (K // 2) + i
            wall[pl.ds(i * chans, chans), :] = lax.dot_general(
                filt[k], cot2[...], (((0,), (0,)), ((), ())), preferred_element_type=F32
            )

        @pl.when(is_polar)
        def _():
            for i in range(K // 2):
                wall[pl.ds(i * chans, chans), :] += lax.dot_general(
                    sw[...].astype(BF16), gw[c * (K // 2) + i].astype(BF16),
                    (((0,), (0,)), ((), ())), preferred_element_type=F32,
                )

    weight_half(1 - core)
    wsend[...] = wall[...].astype(BF16)
    to_core = remote(wsend, wrecv, core_sem.at[0], core_sem.at[1], partner)
    to_core.start()
    weight_half(core)
    piece = half_rows // nq
    to_core.wait_recv()
    summed = wall[...] + wrecv[...].astype(F32)
    half[...] = summed.reshape(nq, piece, chans)
    xs[...] = summed.astype(BF16).reshape(nq, piece, chans)

    def xy_copy(o):
        q, dev = xy_peer(o)
        return remote(xs.at[q], xr.at[o], x_ss.at[o], x_rs.at[o], dev)

    for o in xy_order:
        xy_copy(o).start()
    for copy in cot_halo:
        copy.start()

    for i in range(2):
        pl.semaphore_wait(far_sem.at[i], 1)

    loads[5].wait()
    chunk = 8

    def mix_out(b):
        at = pl.ds(b * chunk * L, chunk * L)
        acc = sum(dot(filt[k, at, :], w[k]) for k in range(K))
        conv_v[pl.ds(b * chunk, chunk)] = acc.reshape(chunk, L, chans).astype(BF16)

    loop(0, rows // chunk, mix_out)
    build(bb, bmat, True)
    @pl.when(is_polar)
    def _():
        start = cyc[...]
        from_lag = lax.broadcasted_iota(jnp.int32, (circle, circle), 0)
        to_lag = lax.broadcasted_iota(jnp.int32, (circle, circle), 1)
        turned = ((from_lag + to_lag) % circle == 0).astype(F32).astype(BF16)
        rev[...] = pltpu.roll(dot(start.astype(BF16), turned), lon * L, 1)
        cyc[...] = pltpu.roll(start, lon * L, 1)
        side = circle // 2
        shift = (side + (mid - z) * 2 * L) % side

        def circulant(src, rows_of, dst, at):
            full = jnp.concatenate([cycle_rows(src, n) for n in rows_of], 0)
            for h in range(2):
                turned_side = pltpu.roll(full[:, h * side : (h + 1) * side], shift, 1)
                dst[h, :, pl.ds(at, side)] = turned_side.astype(BF16)

        for p in range(P_SIZE):
            circulant(cyc, [n * P_SIZE + p for n in range(K * SLAB)], qb, p * side)
        for r in taps:
            circulant(
                rev, [(k * SLAB + r) * P_SIZE + p for k in range(K) for p in range(P_SIZE)], qf, r * side
            )

    loop(1, nq, lambda o: xy_copy(o).wait_recv())
    total = half[me_q]
    for o in range(1, nq):
        total = total + xr[o].astype(F32)

    for p in range(4):
        zs[p] = total[
            (p // 2) * (piece // 2) : (p // 2 + 1) * (piece // 2), (p % 2) * 128 : (p % 2 + 1) * 128
        ].astype(BF16)

    def z_copy(d):
        zz, dev = z_peer(d)
        return remote(zs.at[zz % 4], zr.at[z], z_ss.at[d], z_rs.at[d], dev)

    loop(0, zn - 1, lambda i: z_copy(z_offset(i)).start())
    zr[z] = zs[z % 4]

    @pl.when(is_polar)
    def _():
        for i in fars:
            far_copy(i).wait_recv()
        for i in range(len(spans)):
            rest_core(i).start()

    @pl.when(is_polar)
    def _():
        for i in range(len(spans)):
            rest_core(i).wait_recv()
        side = circle // 2
        held_rows = [cells(slab[r, x_hi]).astype(BF16) for r in range(SLAB + P_SIZE)]

        def share(h):
            front = sum(dot(qf[h, :, r * side : (r + 1) * side], held_rows[r]) for r in range(SLAB))
            back = sum(
                dot(qb[h, :, p * side : (p + 1) * side], held_rows[SLAB + p]) for p in range(P_SIZE)
            )
            return jnp.concatenate([front, back], 0)

        part_s[...] = share(1 - x_hi).astype(BF16)
        part_copy().start()
        own_part[...] = share(x_hi)

    for copy in cot_halo:
        copy.wait_recv()

    def backward(b):
        part = dot(bmat[b], window(c_o, c_l, c_r, b))
        for k in range(K):
            grad[k, pl.ds(b * 64, 64), :] = part[k * 64 : (k + 1) * 64]

    loop(0, blocks, backward)

    loop(0, zn - 1, lambda i: z_copy(z_offset(i)).wait_recv())
    acc = zr[0].astype(F32)
    for s in range(1, zn):
        acc = acc + zr[s].astype(F32)
    za[z % 4] = (acc * F32(1.0 / math.sqrt(total_rows * circle))).astype(BF16)
    hand = (2, 1, zn - 1)

    def za_copy(i):
        dst = za.at[z % 4]
        return remote(dst, dst, za_ss.at[i], za_rs.at[i], z_peer(hand[i])[1])

    for i in range(3):
        za_copy(i).start()

    for i in range(3):
        za_copy(i).wait_recv()
    lines = [jnp.concatenate([za[2 * i].astype(F32), za[2 * i + 1].astype(F32)], 1) for i in range(2)]
    fin[core, me_q] = jnp.concatenate(lines, 0).astype(BF16)

    def xa_copy(o):
        dst = fin.at[core, me_q]
        return remote(dst, dst, xa_ss.at[o], xa_rs.at[o], xy_peer(o)[1])

    for o in xy_order:
        xa_copy(o).start()

    def mix_back(b):
        at = pl.ds(b * chunk * L, chunk * L)
        acc = sum(
            lax.dot_general(
                grad[k, at, :].astype(BF16), w[k], (((1,), (1,)), ((), ())),
                preferred_element_type=F32,
            )
            for k in range(K)
        )
        sg_v[pl.ds(b * chunk, chunk)] = acc.reshape(chunk, L, chans).astype(BF16)

    loop(0, rows // chunk, mix_back)

    @pl.when(is_polar)
    def _():
        part_copy().wait_recv()
        sums = own_part[...] + part_r[...].astype(F32)
        front, extra = sums[: K * P_SIZE * L], sums[K * P_SIZE * L :]
        out = sum(dot(front[k * 16 : (k + 1) * 16].astype(BF16), w[k]) for k in range(K))
        conv_v[pl.ds(pole_at, P_SIZE)] = out.reshape(P_SIZE, L, chans).astype(BF16)
        at = pl.multiple_of(slab_at * L, 8)
        back = sum(
            lax.dot_general(
                (grad[k, pl.ds(at, SLAB * L), :] + extra[k * SLAB * L : (k + 1) * SLAB * L]).astype(BF16),
                w[k], (((1,), (1,)), ((), ())), preferred_element_type=F32,
            )
            for k in range(K)
        )
        sg_v[pl.ds(slab_at, SLAB)] = back.reshape(SLAB, L, chans).astype(BF16)

    sg_copy = pltpu.make_async_copy(sg_v, sgrad_out, out_sem.at[1])
    sg_copy.start()
    conv_copy = pltpu.make_async_copy(conv_v, conv_out, out_sem.at[0])
    conv_copy.start()

    def column(c, dx):
        return fin.at[c, pl.ds((x - dx + XS) % XS * ys, ys)]

    def swap(i, dx):
        part = column(core, dx)
        return remote(part, part, fc_ss.at[i], fc_rs.at[i], partner)

    def leave(i, c, dx):
        dst = wgrad_out.at[c, pl.ds((x - dx + XS) % XS * ys, ys)]
        return pltpu.make_async_copy(column(c, dx), dst, out_sem.at[i])

    columns = list(enumerate((0, 1, XS - 1, 2)))
    for i, dx in columns:
        for o in range(dx * ys, (dx + 1) * ys):
            if o > 0:
                xa_copy(o).wait_recv()
        swap(i, dx).start()
        leave(2 + i, core, dx).start()

    @pl.when(is_polar)
    def _():
        for d in near_order:
            near_z(d).wait_send()
        for d in [0] + near_order:
            cot_x(d).wait_send()
        cot_core().wait_send()
        for i in fars:
            far_copy(i).wait_send()
        for i in range(len(spans)):
            rest_core(i).wait_send()
        part_copy().wait_send()

    for copy in sig_halo + cot_halo:
        copy.wait_send()
    to_core.wait_send()
    loop(1, nq, lambda o: xy_copy(o).wait_send())
    loop(1, zn, lambda d: z_copy(d).wait_send())
    for i in range(3):
        za_copy(i).wait_send()
    loop(1, nq, lambda o: xa_copy(o).wait_send())
    conv_copy.wait()
    sg_copy.wait()
    for i, dx in columns:
        swap(i, dx).wait()
        leave(2 + XS + i, 1 - core, dx).start()
    for i, dx in columns:
        leave(2 + i, core, dx).wait()
        leave(2 + XS + i, 1 - core, dx).wait()


def finish(conv, sgrad, wgrad):
    parts = 4

    def body(conv_in, sg_in, wg_in, conv_out, sg_out, wg_out, held, wide, fields, sems):
        ends = [(conv_in, fields.at[0], conv_out), (sg_in, fields.at[1], sg_out)]
        ends += [(wg_in.at[k], held.at[k], wg_out.at[k]) for k in range(parts)]
        loads = [pltpu.make_async_copy(a, b, sems.at[0, i]) for i, (a, b, _) in enumerate(ends)]
        stores = [
            pltpu.make_async_copy(b if i < 2 else wide.at[i - 2], c, sems.at[1, i])
            for i, (_, b, c) in enumerate(ends)
        ]
        for copy in loads:
            copy.start()
        for i in range(2 + parts):
            loads[i].wait()
            if i >= 2:
                wide[i - 2] = held[i - 2].astype(F32)
            stores[i].start()
        for copy in stores:
            copy.wait()

    return pl.pallas_call(
        body,
        out_shape=(
            jax.ShapeDtypeStruct(conv.shape, conv.dtype),
            jax.ShapeDtypeStruct(sgrad.shape, sgrad.dtype),
            jax.ShapeDtypeStruct(wgrad.shape, F32),
        ),
        in_specs=[pl.BlockSpec(memory_space=pl.ANY)] * 3,
        out_specs=[pl.BlockSpec(memory_space=pl.ANY)] * 3,
        scratch_shapes=[
            pltpu.VMEM(wgrad.shape, BF16), pltpu.VMEM(wgrad.shape, F32),
            pltpu.VMEM((2,) + conv.shape, BF16), pltpu.SemaphoreType.DMA((2, 2 + parts)),
        ],
        compiler_params=pltpu.CompilerParams(vmem_limit_bytes=60 * 2**20),
    )(conv, sgrad, wgrad)


def local(signal, cotangent, weights, band_kernel, cycle_kernel, support_width):
    rows, _, chans = signal.shape
    nlat, nlon = lax.axis_size("lat"), lax.axis_size("lon")
    ys, zn = nlat // X_LO, nlon // (2 * X_HI)
    nq = XS * ys
    circle = nlon * L
    blocks, cells = rows // 8, rows * L
    half_rows = K * chans // 2
    piece = half_rows // nq
    band = band_kernel.transpose(2, 3, 0, 1)
    cycle = cycle_kernel.transpose(0, 2, 1, 3)
    dma = pltpu.SemaphoreType.DMA
    ext = (rows + 2, L, chans)
    base = pltpu.VMEM((K, rows, 256), F32)
    turns = pltpu.VMEM((K * SLAB * P_SIZE, circle), F32)
    matrices = pltpu.VMEM((blocks, K * 64, 256), BF16)
    scratch = (
        [pltpu.VMEM(ext, BF16)] * 6
        + [pltpu.VMEM(weights.shape, BF16)]
        + [pltpu.VMEM(band.shape, BF16)]
        + [pltpu.VMEM((K, 2 * R + 1, 2 * P_SIZE, circle), BF16)]
        + [pltpu.SMEM(support_width.shape, jnp.int32)]
        + [pltpu.VMEM((256, rows * nlat), F32), pltpu.VMEM((rows * nlat + 32, 256), BF16)]
        + [base] * 2 + [turns] * 2 + [matrices] * 2
        + [pltpu.VMEM((K, cells, chans), BF16), pltpu.VMEM((K, cells, chans), F32)]
        + [pltpu.VMEM((cells, chans), BF16)]
        + [pltpu.VMEM((rows, L, chans), BF16)] * 2
        + [pltpu.VMEM((SLAB + P_SIZE, X_HI, zn, 2, L, chans), BF16)]
        + [pltpu.VMEM((2, K * P_SIZE * L, SLAB * circle // 2), BF16)]
        + [pltpu.VMEM((2, K * SLAB * L, P_SIZE * circle // 2), BF16)]
        + [pltpu.VMEM((P_SIZE, K * SLAB * L, circle), BF16)]
        + [pltpu.VMEM((K, zn // 2 * SLAB * L, chans), F32), pltpu.VMEM((zn // 2 * SLAB * L, chans), F32)]
        + [pltpu.VMEM((K * (P_SIZE + SLAB) * L, chans), BF16)] * 2
        + [pltpu.VMEM((K * (P_SIZE + SLAB) * L, chans), F32)]
        + [pltpu.VMEM((half_rows, chans), F32)]
        + [pltpu.VMEM((half_rows, chans), BF16)] * 2
        + [pltpu.VMEM((nq, piece, chans), F32)]
        + [pltpu.VMEM((nq, piece, chans), BF16)] * 2
        + [pltpu.VMEM((n, piece // 2, 128), BF16) for n in (4, zn, 4)]
        + [pltpu.VMEM((2, nq, piece, chans), BF16)]
        + [pltpu.SemaphoreType.REGULAR((2,))]
        + [dma((n,)) for n in (
            6, 16, 16, 2, zn, zn, zn, zn, 2,
            2, 2, 3, 3, 2,
            2, nq, nq, zn, zn, 3, 3, nq, nq, XS, XS, 2 + 2 * XS,
        )]
    )
    field = jax.ShapeDtypeStruct(signal.shape, BF16)
    conv, sgrad, wgrad = pl.pallas_call(
        kernel,
        out_shape=(field, field, jax.ShapeDtypeStruct((2, nq, piece, chans), BF16)),
        in_specs=[pl.BlockSpec(memory_space=pl.ANY)] * 6,
        out_specs=[pl.BlockSpec(memory_space=pl.ANY)] * 3,
        scratch_shapes=scratch,
        compiler_params=pltpu.CompilerParams(
            collective_id=0, has_side_effects=True, vmem_limit_bytes=60 * 2**20
        ),
        cost_estimate=pl.CostEstimate(flops=10**9, bytes_accessed=4 * 10**6, transcendentals=0),
    )(signal, cotangent, weights, band, cycle, support_width)
    return finish(conv, sgrad, wgrad.reshape(K, chans, chans))


def solution(mesh):
    placed = (P("lat", "lon", None), P("lat", "lon", None), P(), P(), P(), P())
    return jax.shard_map(
        local,
        mesh=mesh,
        in_specs=placed,
        out_specs=(P("lat", "lon", None), P("lat", "lon", None), P()),
        check_vma=False,
    )
```

```python
import functools
import math

import jax
import jax.numpy as jnp
from jax import lax
from jax.experimental import pallas as pl
from jax.experimental.pallas import tpu as pltpu
from jax.sharding import PartitionSpec as P

K = 4
R = 1
H = 8
P_SIZE = 2
L = 8
SLAB = P_SIZE + R
X_HI = 2
X_LO = 2
XS = X_HI * X_LO
MESH = pl.DeviceIdType.MESH
F32 = jnp.float32
BF16 = jnp.bfloat16


def dot(a, b):
    return jnp.dot(a, b, preferred_element_type=F32)


def kernel(
    sig, cot, w_hbm, band_hbm, cycle_hbm, width_hbm,
    conv_out, sgrad_out, wgrad_out,
    s_o, s_l, s_r, c_o, c_l, c_r, w, band, circ, width, taps_v, taps_t,
    bf, bb, cyc, rev, amat, bmat, filt, grad, cot2, conv_v, sg_v,
    slab, qf, qb, qt, gw, sw, part_s, part_r, own_part,
    wall, wsend, wrecv, half, xs, xr, zs, zr, za, fin,
    far_sem, load_sem, halo_ss, halo_rs, own_sem, pc_ss, pc_rs, px_ss, px_rs, pk_sem,
    ps_ss, ps_rs, pb_ss, pb_rs, pp_sem,
    core_sem, x_ss, x_rs, z_ss, z_rs, za_ss, za_rs, xa_ss, xa_rs, fc_ss, fc_rs, out_sem,
):
    rows, _, chans = sig.shape
    nlat, nlon = lax.axis_size("lat"), lax.axis_size("lon")
    ys, zn = nlat // X_LO, nlon // (2 * X_HI)
    lat, lon = lax.axis_index("lat"), lax.axis_index("lon")
    x_lo, y = lat // ys, lat % ys
    x_hi, z, core = lon // (2 * zn), (lon // 2) % zn, lon % 2
    x = x_hi * X_LO + x_lo
    me_q = x * ys + y
    nq = XS * ys
    blocks = rows // 8
    circle = nlon * L
    first_row, total_rows = lat * rows, rows * nlat
    is_top = lat == 0
    is_polar = is_top | (lat == nlat - 1)

    def place(xx, yy, zz, cc):
        return {"lat": (xx % X_LO) * ys + yy, "lon": (xx // X_LO) * (2 * zn) + zz * 2 + cc}

    def reach(o):
        dx, dy = o // ys, o % ys
        return min(dx, XS - dx) + min(dy, ys - dy)

    xy_order = sorted(range(1, nq), key=lambda o: -reach(o))

    near, mid = zn // 4, zn // 2

    def z_offset(i):
        return mid + (1 - 2 * (i % 2)) * ((i + 1) // 2)

    near_order = [d for n in range(near, 0, -1) for d in (n, zn - n)]

    def xy_peer(o):
        xx, yy = (x + o // ys) % XS, (y + o % ys) % ys
        return xx * ys + yy, place(xx, yy, z, core)

    def z_peer(d):
        zz = (z + d) % zn
        return zz, place(x, y, zz, core)

    def beside(dlat, dlon):
        return {"lat": (lat + dlat + nlat) % nlat, "lon": (lon + dlon + nlon) % nlon}

    partner = place(x, y, z, 1 - core)
    x_other = place((x + X_LO) % XS, y, z, core)

    def remote(src, dst, ss, rs, dev):
        return pltpu.make_async_remote_copy(
            src_ref=src, dst_ref=dst, send_sem=ss, recv_sem=rs, device_id=dev, device_id_type=MESH
        )

    def loop(lo, hi, f):
        def body(i, c):
            f(i)
            return c

        lax.fori_loop(lo, hi, body, 0)

    barrier = pltpu.get_barrier_semaphore()

    def greet(dev):
        pl.semaphore_signal(barrier, inc=1, device_id=dev, device_id_type=MESH)

    @pl.when(is_polar)
    def _():
        for d in near_order:
            greet(place((x + X_LO) % XS, y, (z + d) % zn, core))

    for d in near_order:
        greet(z_peer(d)[1])
    for o in xy_order:
        greet(xy_peer(o)[1])
    for dlat, dlon in ((1, 1), (1, -1), (-1, 1), (-1, -1), (0, 1), (0, -1)):
        greet(beside(dlat, dlon))

    loads = [
        pltpu.make_async_copy(a, b, load_sem.at[i])
        for i, (a, b) in enumerate((
            (band_hbm, band),
            (width_hbm, width),
            (cycle_hbm, circ),
            (sig, s_o.at[pl.ds(1, rows)]),
            (cot, c_o.at[pl.ds(1, rows)]),
            (w_hbm, w),
        ))
    ]
    slab_at = jnp.where(is_top, 0, rows - SLAB)
    pole_at = jnp.where(is_top, 0, rows - P_SIZE)
    sig_slab = sig.at[pl.ds(slab_at, SLAB)]
    cot_slab = cot.at[pl.ds(pole_at, P_SIZE)]
    sig_rows, cot_rows = pl.ds(0, SLAB), pl.ds(SLAB, P_SIZE)

    def seen(d):
        return mid - d if d <= mid else mid + zn - d

    def near_z(d):
        src = slab.at[:, x_hi, mid, core]
        dst = slab.at[:, x_hi, seen(d), core]
        return remote(src, dst, pc_ss.at[d], pc_rs.at[d], z_peer(d)[1])

    def cot_x(d):
        dst = slab.at[cot_rows, x_hi, seen(d), core]
        dev = place((x + X_LO) % XS, y, (z + d) % zn, core)
        src = slab.at[cot_rows, x_hi, mid, core]
        return remote(src, dst, px_ss.at[d], px_rs.at[d], dev)

    def cot_core():
        part = slab.at[cot_rows, :, pl.ds(mid - near, 2 * near + 1), core]
        return remote(part, part, pk_sem.at[0], pk_sem.at[1], partner)

    def far_copy(i):
        src, dst, n, d = (
            (mid - near, 0, near, near), (mid + 1, mid + near + 1, near - 1, zn - near)
        )[i]
        return remote(
            slab.at[:, x_hi, pl.ds(src, n), core], slab.at[:, x_hi, pl.ds(dst, n), core],
            ps_ss.at[i], ps_rs.at[i], z_peer(d)[1],
        )

    fars = [0, 1] if near > 1 else [0]
    spans = [(cot_rows, 0, mid - near), (cot_rows, mid + near + 1, mid - near - 1), (sig_rows, 0, zn)]
    spans = [span for span in spans if span[2] > 0]

    def rest_core(i):
        held, lo, n = spans[i]
        part = slab.at[held, x_hi, pl.ds(lo, n), core]
        return remote(part, part, pb_ss.at[i], pb_rs.at[i], partner)

    def part_copy():
        return remote(part_s, part_r, pp_sem.at[0], pp_sem.at[1], x_other)

    own_slab = [
        pltpu.make_async_copy(cot_slab, slab.at[cot_rows, x_hi, mid, core], own_sem.at[0]),
        pltpu.make_async_copy(sig_slab, slab.at[sig_rows, x_hi, mid, core], own_sem.at[1]),
    ]

    @pl.when(is_polar)
    def _():
        for copy in own_slab:
            copy.start()

    for copy in loads[:4]:
        copy.start()

    @pl.when(is_polar)
    def _():
        for copy in own_slab:
            copy.wait()

    greeted = 6 + (nq - 1) + 2 * near
    pl.semaphore_wait(barrier, jnp.where(is_polar, greeted + 2 * near, greeted))
    for i, d in enumerate((near, zn - near)):
        pl.semaphore_signal(far_sem.at[i], inc=1, device_id=z_peer(d)[1], device_id_type=MESH)

    @pl.when(is_polar)
    def _():
        for d in near_order:
            cot_x(d).start()
            near_z(d).start()
        cot_x(0).start()

    def halo_copies(src, own, left, right, n):
        last, first = src.at[pl.ds(rows - 1, 1)], src.at[pl.ds(0, 1)]
        top, bottom = pl.ds(0, 1), pl.ds(rows + 1, 1)
        spec = (
            (last, left.at[top], beside(1, 1)),
            (last, right.at[top], beside(1, -1)),
            (first, left.at[bottom], beside(-1, 1)),
            (first, right.at[bottom], beside(-1, -1)),
            (last, own.at[top], beside(1, 0)),
            (first, own.at[bottom], beside(-1, 0)),
            (src, left.at[pl.ds(1, rows)], beside(0, 1)),
            (src, right.at[pl.ds(1, rows)], beside(0, -1)),
        )
        return [
            remote(a, b, halo_ss.at[n + i], halo_rs.at[n + i], dev)
            for i, (a, b, dev) in enumerate(spec)
        ]

    sig_halo = halo_copies(sig, s_o, s_l, s_r, 0)
    cot_halo = halo_copies(cot, c_o, c_l, c_r, 8)
    for copy in sig_halo:
        copy.start()
    for copy in loads[4:]:
        copy.start()

    loads[0].wait()
    loads[1].wait()
    lanes = 256
    taps = range(2 * R + 1)
    lags = 2 * H + 1
    used = (2 * R + 1) * lags * K
    taps_v[...] = jnp.zeros_like(taps_v)
    for r in taps:
        for d in range(lags):
            taps_v[pl.ds((r * lags + d) * K, K), :] = band[r, d].astype(F32)
    taps_t[pl.ds(0, 16), :] = jnp.zeros((16, lanes), BF16)
    taps_t[pl.ds(16, total_rows), :] = jnp.transpose(taps_v[...])[:total_rows].astype(BF16)
    taps_t[pl.ds(16 + total_rows, 16), :] = jnp.zeros((16, lanes), BF16)
    mine = taps_t[pl.ds(pl.multiple_of(first_row, 16), rows + 32), :]
    held = lax.broadcasted_iota(jnp.int32, (lanes, 1), 0)
    held_k, held_r, held_d = held % K, held // (K * lags), held // K % lags
    lane = lax.broadcasted_iota(jnp.int32, (lanes, lanes), 1)
    to_f = jnp.where(held < used, held_r * 3 * L + 2 * H - held_d, -1)
    to_b = jnp.where(held < used, (2 * R - held_r) * 3 * L + held_d, -1)
    for k in range(K):
        placed = [
            dot(mine, (lane == jnp.where(held_k == k, to, -1)).astype(F32).astype(BF16))
            for to in (to_f, to_b)
        ]
        bf[k] = placed[0][16 : 16 + rows]
        slots = lax.broadcasted_iota(jnp.int32, (1, lanes), 1) // (3 * L)
        above, same, below = (placed[1][15 + s : 15 + s + rows] for s in taps)
        bb[k] = jnp.where(slots == 0, above, jnp.where(slots == 1, same, below))
    lane_row = lax.broadcasted_iota(jnp.int32, (1, lanes), 1)
    slot = lane_row // (3 * L)
    away = jnp.abs(lane_row - slot * (3 * L) - H)

    def width_of(i):
        row = first_row + i
        held = width[(row + total_rows) % total_rows]
        return jnp.where((row >= P_SIZE) & (row < total_rows - P_SIZE), held, -1)

    def build(src, dst, backward):
        def block(b):
            allowed = []
            for i in range(8):
                row = b * 8 + i
                if backward:
                    near = [width_of(row + s - R) for s in taps]
                    limit = jnp.where(slot == 0, near[0], jnp.where(slot == 1, near[1], near[2]))
                else:
                    limit = width_of(row)
                allowed.append(away <= limit)
            for k in range(K):
                tile = src[k, pl.ds(pl.multiple_of(b * 8, 8), 8), :]
                for i in range(0, 8, 2):
                    parts = [
                        pltpu.roll(
                            jnp.broadcast_to(jnp.where(allowed[j], tile[j : j + 1], 0.0), (L, lanes)),
                            j * 3 * L, 1, stride=1, stride_axis=0,
                        )
                        for j in (i, i + 1)
                    ]
                    dst[b, pl.ds((k * 8 + i) * L, 2 * L), :] = jnp.concatenate(parts, 0).astype(BF16)

        loop(0, blocks, block)

    def window(o, left, right, b):
        at = pl.ds(b * 8, 10)
        parts = [ref[at].astype(F32) for ref in (left, o, right)]
        both = jnp.concatenate(parts, 1).reshape(30 * L, chans)
        return jnp.concatenate([both, jnp.zeros((2 * L, chans), F32)], 0).astype(BF16)

    build(bf, amat, False)

    loads[2].wait()

    def cycle_rows(src, r):
        row = jnp.broadcast_to(src[r : r + 1, :], (L, circle))
        return pltpu.roll(row, 0, 1, stride=1, stride_axis=0)

    @pl.when(is_polar)
    def _():
        none = jnp.zeros((1, circle), F32)
        for k in range(K):
            for p in range(P_SIZE):

                def tap(r):
                    if not 0 <= r <= 2 * R:
                        return none
                    held = circ[k, r].astype(F32)
                    return jnp.where(is_top, held[p : p + 1], held[P_SIZE + p : P_SIZE + p + 1])

                for r in taps:
                    at = (k * SLAB + r) * P_SIZE + p
                    cyc[at : at + 1, :] = jnp.where(is_top, tap(r - p + R), tap(r - p))
        col = lax.broadcasted_iota(jnp.int32, (1, circle), 1)
        t, c = col // (8 * L) - near, col % (8 * L)
        xh, o, cc, l = c // (4 * L), c // (2 * L) % 2, c // L % 2, c % L
        z_cot, z_sig = (z + t + o + zn) % zn, (z - t + zn) % zn
        lag = (xh - x_hi) * (circle // 2) + (z_cot - z_sig) * (2 * L) + (cc - core) * L + l
        lag = (lag + 2 * circle) % circle
        pick = (lax.broadcasted_iota(jnp.int32, (circle, circle), 0) == lag).astype(F32).astype(BF16)
        for p in range(P_SIZE):
            turned = [cycle_rows(cyc, n * P_SIZE + p) for n in range(K * SLAB)]
            qt[p] = dot(jnp.concatenate(turned, 0).astype(BF16), pick).astype(BF16)
        for d in [0] + near_order:
            cot_x(d).wait_recv()
        for d in near_order:
            near_z(d).wait_recv()
        cot_core().start()

    loads[3].wait()
    for copy in sig_halo:
        copy.wait_recv()
    @pl.when(is_polar)
    def _():
        for i in fars:
            far_copy(i).start()

    def forward(b):
        part = dot(amat[b], window(s_o, s_l, s_r, b)).astype(BF16)
        for k in range(K):
            filt[k, pl.ds(b * 64, 64), :] = part[k * 64 : (k + 1) * 64]

    loop(0, blocks, forward)
    loads[4].wait()

    def fold(b):
        cot2[pl.ds(b * 64, 64), :] = (
            c_o[pl.ds(1 + b * 8, 8)].astype(F32).reshape(64, chans).astype(BF16)
        )

    loop(0, blocks, fold)

    def cells(ref):
        held = ref.astype(F32)
        return held.reshape(-1, chans)

    @pl.when(is_polar)
    def _():
        cot_core().wait_recv()
        for i in range(2 * near):
            t = i - near
            turned = sum(
                dot(
                    qt[p, :, i * 8 * L : (i + 1) * 8 * L],
                    cells(slab[SLAB + p, :, mid + t : mid + t + 2]).astype(BF16),
                )
                for p in range(P_SIZE)
            )
            for k in range(K):
                gw[k, pl.ds(i * SLAB * L, SLAB * L), :] = turned[k * SLAB * L : (k + 1) * SLAB * L]
            sw[pl.ds(i * SLAB * L, SLAB * L), :] = cells(slab[0:SLAB, x_hi, mid - t, core])
    half_rows = K * chans // 2

    def weight_part(c, i):
        k = c * (K // 2) + i
        at = pl.ds(i * chans, chans)
        wall[at, :] = lax.dot_general(
            filt[k], cot2[...], (((0,), (0,)), ((), ())), preferred_element_type=F32
        )

        @pl.when(is_polar)
        def _():
            wall[at, :] += lax.dot_general(
                sw[...].astype(BF16), gw[k].astype(BF16),
                (((0,), (0,)), ((), ())), preferred_element_type=F32,
            )

    def to_core(i):
        at = pl.ds(i * chans, chans)
        return remote(wsend.at[at], wrecv.at[at], core_sem.at[i], core_sem.at[K // 2 + i], partner)

    for i in range(K // 2):
        weight_part(1 - core, i)
        at = pl.ds(i * chans, chans)
        wsend[at, :] = wall[at, :].astype(BF16)
        to_core(i).start()
    for i in range(K // 2):
        weight_part(core, i)
    piece = half_rows // nq
    for i in range(K // 2):
        to_core(i).wait_recv()
    summed = wall[...] + wrecv[...].astype(F32)
    half[...] = summed.reshape(nq, piece, chans)
    xs[...] = summed.astype(BF16).reshape(nq, piece, chans)

    def xy_copy(o):
        q, dev = xy_peer(o)
        return remote(xs.at[q], xr.at[o], x_ss.at[o], x_rs.at[o], dev)

    for o in xy_order:
        xy_copy(o).start()
    for copy in cot_halo:
        copy.start()

    for i in range(2):
        pl.semaphore_wait(far_sem.at[i], 1)

    loads[5].wait()
    chunk = 8

    def mix_out(b):
        at = pl.ds(b * chunk * L, chunk * L)
        acc = sum(dot(filt[k, at, :], w[k]) for k in range(K))
        conv_v[pl.ds(b * chunk, chunk)] = acc.reshape(chunk, L, chans).astype(BF16)

    loop(0, rows // chunk, mix_out)
    build(bb, bmat, True)
    @pl.when(is_polar)
    def _():
        start = cyc[...]
        from_lag = lax.broadcasted_iota(jnp.int32, (circle, circle), 0)
        to_lag = lax.broadcasted_iota(jnp.int32, (circle, circle), 1)
        turned = ((from_lag + to_lag) % circle == 0).astype(F32).astype(BF16)
        rev[...] = pltpu.roll(dot(start.astype(BF16), turned), lon * L, 1)
        cyc[...] = pltpu.roll(start, lon * L, 1)
        side = circle // 2
        shift = (side + (mid - z) * 2 * L) % side

        def circulant(src, rows_of, dst, at):
            full = jnp.concatenate([cycle_rows(src, n) for n in rows_of], 0)
            for h in range(2):
                turned_side = pltpu.roll(full[:, h * side : (h + 1) * side], shift, 1)
                dst[h, :, pl.ds(at, side)] = turned_side.astype(BF16)

        for p in range(P_SIZE):
            circulant(cyc, [n * P_SIZE + p for n in range(K * SLAB)], qb, p * side)
        for r in taps:
            circulant(
                rev, [(k * SLAB + r) * P_SIZE + p for k in range(K) for p in range(P_SIZE)], qf, r * side
            )

    loop(1, nq, lambda o: xy_copy(o).wait_recv())
    total = half[me_q]
    for o in range(1, nq):
        total = total + xr[o].astype(F32)

    for p in range(4):
        zs[p] = total[
            (p // 2) * (piece // 2) : (p // 2 + 1) * (piece // 2), (p % 2) * 128 : (p % 2 + 1) * 128
        ].astype(BF16)

    def z_copy(d):
        zz, dev = z_peer(d)
        return remote(zs.at[zz % 4], zr.at[z], z_ss.at[d], z_rs.at[d], dev)

    loop(0, zn - 1, lambda i: z_copy(z_offset(i)).start())
    zr[z] = zs[z % 4]

    @pl.when(is_polar)
    def _():
        for i in fars:
            far_copy(i).wait_recv()
        for i in range(len(spans)):
            rest_core(i).start()

    @pl.when(is_polar)
    def _():
        for i in range(len(spans)):
            rest_core(i).wait_recv()
        side = circle // 2
        held_rows = [cells(slab[r, x_hi]).astype(BF16) for r in range(SLAB + P_SIZE)]

        def share(h):
            front = sum(dot(qf[h, :, r * side : (r + 1) * side], held_rows[r]) for r in range(SLAB))
            back = sum(
                dot(qb[h, :, p * side : (p + 1) * side], held_rows[SLAB + p]) for p in range(P_SIZE)
            )
            return jnp.concatenate([front, back], 0)

        part_s[...] = share(1 - x_hi).astype(BF16)
        part_copy().start()
        own_part[...] = share(x_hi)

    for copy in cot_halo:
        copy.wait_recv()

    def backward(b):
        part = dot(bmat[b], window(c_o, c_l, c_r, b))
        for k in range(K):
            grad[k, pl.ds(b * 64, 64), :] = part[k * 64 : (k + 1) * 64]

    loop(0, blocks, backward)

    loop(0, zn - 1, lambda i: z_copy(z_offset(i)).wait_recv())
    acc = zr[0].astype(F32)
    for s in range(1, zn):
        acc = acc + zr[s].astype(F32)
    za[z % 4] = (acc * F32(1.0 / math.sqrt(total_rows * circle))).astype(BF16)
    hand = (2, 1, zn - 1)

    def za_copy(i):
        dst = za.at[z % 4]
        return remote(dst, dst, za_ss.at[i], za_rs.at[i], z_peer(hand[i])[1])

    for i in range(3):
        za_copy(i).start()

    for i in range(3):
        za_copy(i).wait_recv()
    lines = [jnp.concatenate([za[2 * i].astype(F32), za[2 * i + 1].astype(F32)], 1) for i in range(2)]
    fin[core, me_q] = jnp.concatenate(lines, 0).astype(BF16)

    def xa_copy(o):
        dst = fin.at[core, me_q]
        return remote(dst, dst, xa_ss.at[o], xa_rs.at[o], xy_peer(o)[1])

    for o in xy_order:
        xa_copy(o).start()

    def mix_back(b):
        at = pl.ds(b * chunk * L, chunk * L)
        acc = sum(
            lax.dot_general(
                grad[k, at, :].astype(BF16), w[k], (((1,), (1,)), ((), ())),
                preferred_element_type=F32,
            )
            for k in range(K)
        )
        sg_v[pl.ds(b * chunk, chunk)] = acc.reshape(chunk, L, chans).astype(BF16)

    loop(0, rows // chunk, mix_back)

    @pl.when(is_polar)
    def _():
        part_copy().wait_recv()
        sums = own_part[...] + part_r[...].astype(F32)
        front, extra = sums[: K * P_SIZE * L], sums[K * P_SIZE * L :]
        out = sum(dot(front[k * 16 : (k + 1) * 16].astype(BF16), w[k]) for k in range(K))
        conv_v[pl.ds(pole_at, P_SIZE)] = out.reshape(P_SIZE, L, chans).astype(BF16)
        at = pl.multiple_of(slab_at * L, 8)
        back = sum(
            lax.dot_general(
                (grad[k, pl.ds(at, SLAB * L), :] + extra[k * SLAB * L : (k + 1) * SLAB * L]).astype(BF16),
                w[k], (((1,), (1,)), ((), ())), preferred_element_type=F32,
            )
            for k in range(K)
        )
        sg_v[pl.ds(slab_at, SLAB)] = back.reshape(SLAB, L, chans).astype(BF16)

    sg_copy = pltpu.make_async_copy(sg_v, sgrad_out, out_sem.at[1])
    sg_copy.start()
    conv_copy = pltpu.make_async_copy(conv_v, conv_out, out_sem.at[0])
    conv_copy.start()

    def column(c, dx):
        return fin.at[c, pl.ds((x - dx + XS) % XS * ys, ys)]

    def swap(i, dx):
        part = column(core, dx)
        return remote(part, part, fc_ss.at[i], fc_rs.at[i], partner)

    def leave(i, c, dx):
        dst = wgrad_out.at[c, pl.ds((x - dx + XS) % XS * ys, ys)]
        return pltpu.make_async_copy(column(c, dx), dst, out_sem.at[i])

    columns = list(enumerate((0, 1, XS - 1, 2)))
    for i, dx in columns:
        for o in range(dx * ys, (dx + 1) * ys):
            if o > 0:
                xa_copy(o).wait_recv()
        swap(i, dx).start()
        leave(2 + i, core, dx).start()

    @pl.when(is_polar)
    def _():
        for d in near_order:
            near_z(d).wait_send()
        for d in [0] + near_order:
            cot_x(d).wait_send()
        cot_core().wait_send()
        for i in fars:
            far_copy(i).wait_send()
        for i in range(len(spans)):
            rest_core(i).wait_send()
        part_copy().wait_send()

    for copy in sig_halo + cot_halo:
        copy.wait_send()
    for i in range(K // 2):
        to_core(i).wait_send()
    loop(1, nq, lambda o: xy_copy(o).wait_send())
    loop(1, zn, lambda d: z_copy(d).wait_send())
    for i in range(3):
        za_copy(i).wait_send()
    loop(1, nq, lambda o: xa_copy(o).wait_send())
    conv_copy.wait()
    sg_copy.wait()
    for i, dx in columns:
        swap(i, dx).wait()
        leave(2 + XS + i, 1 - core, dx).start()
    for i, dx in columns:
        leave(2 + i, core, dx).wait()
        leave(2 + XS + i, 1 - core, dx).wait()


def finish(conv, sgrad, wgrad):
    parts = 4

    def body(conv_in, sg_in, wg_in, conv_out, sg_out, wg_out, held, wide, fields, sems):
        ends = [(conv_in, fields.at[0], conv_out), (sg_in, fields.at[1], sg_out)]
        ends += [(wg_in.at[k], held.at[k], wg_out.at[k]) for k in range(parts)]
        loads = [pltpu.make_async_copy(a, b, sems.at[0, i]) for i, (a, b, _) in enumerate(ends)]
        stores = [
            pltpu.make_async_copy(b if i < 2 else wide.at[i - 2], c, sems.at[1, i])
            for i, (_, b, c) in enumerate(ends)
        ]
        for copy in loads:
            copy.start()
        for i in range(2 + parts):
            loads[i].wait()
            if i >= 2:
                wide[i - 2] = held[i - 2].astype(F32)
            stores[i].start()
        for copy in stores:
            copy.wait()

    return pl.pallas_call(
        body,
        out_shape=(
            jax.ShapeDtypeStruct(conv.shape, conv.dtype),
            jax.ShapeDtypeStruct(sgrad.shape, sgrad.dtype),
            jax.ShapeDtypeStruct(wgrad.shape, F32),
        ),
        in_specs=[pl.BlockSpec(memory_space=pl.ANY)] * 3,
        out_specs=[pl.BlockSpec(memory_space=pl.ANY)] * 3,
        scratch_shapes=[
            pltpu.VMEM(wgrad.shape, BF16), pltpu.VMEM(wgrad.shape, F32),
            pltpu.VMEM((2,) + conv.shape, BF16), pltpu.SemaphoreType.DMA((2, 2 + parts)),
        ],
        compiler_params=pltpu.CompilerParams(vmem_limit_bytes=60 * 2**20),
    )(conv, sgrad, wgrad)


def local(signal, cotangent, weights, band_kernel, cycle_kernel, support_width):
    rows, _, chans = signal.shape
    nlat, nlon = lax.axis_size("lat"), lax.axis_size("lon")
    ys, zn = nlat // X_LO, nlon // (2 * X_HI)
    nq = XS * ys
    circle = nlon * L
    blocks, cells = rows // 8, rows * L
    half_rows = K * chans // 2
    piece = half_rows // nq
    band = band_kernel.transpose(2, 3, 0, 1)
    cycle = cycle_kernel.transpose(0, 2, 1, 3)
    dma = pltpu.SemaphoreType.DMA
    ext = (rows + 2, L, chans)
    base = pltpu.VMEM((K, rows, 256), F32)
    turns = pltpu.VMEM((K * SLAB * P_SIZE, circle), F32)
    matrices = pltpu.VMEM((blocks, K * 64, 256), BF16)
    scratch = (
        [pltpu.VMEM(ext, BF16)] * 6
        + [pltpu.VMEM(weights.shape, BF16)]
        + [pltpu.VMEM(band.shape, BF16)]
        + [pltpu.VMEM((K, 2 * R + 1, 2 * P_SIZE, circle), BF16)]
        + [pltpu.SMEM(support_width.shape, jnp.int32)]
        + [pltpu.VMEM((256, rows * nlat), F32), pltpu.VMEM((rows * nlat + 32, 256), BF16)]
        + [base] * 2 + [turns] * 2 + [matrices] * 2
        + [pltpu.VMEM((K, cells, chans), BF16), pltpu.VMEM((K, cells, chans), F32)]
        + [pltpu.VMEM((cells, chans), BF16)]
        + [pltpu.VMEM((rows, L, chans), BF16)] * 2
        + [pltpu.VMEM((SLAB + P_SIZE, X_HI, zn, 2, L, chans), BF16)]
        + [pltpu.VMEM((2, K * P_SIZE * L, SLAB * circle // 2), BF16)]
        + [pltpu.VMEM((2, K * SLAB * L, P_SIZE * circle // 2), BF16)]
        + [pltpu.VMEM((P_SIZE, K * SLAB * L, circle), BF16)]
        + [pltpu.VMEM((K, zn // 2 * SLAB * L, chans), F32), pltpu.VMEM((zn // 2 * SLAB * L, chans), F32)]
        + [pltpu.VMEM((K * (P_SIZE + SLAB) * L, chans), BF16)] * 2
        + [pltpu.VMEM((K * (P_SIZE + SLAB) * L, chans), F32)]
        + [pltpu.VMEM((half_rows, chans), F32)]
        + [pltpu.VMEM((half_rows, chans), BF16)] * 2
        + [pltpu.VMEM((nq, piece, chans), F32)]
        + [pltpu.VMEM((nq, piece, chans), BF16)] * 2
        + [pltpu.VMEM((n, piece // 2, 128), BF16) for n in (4, zn, 4)]
        + [pltpu.VMEM((2, nq, piece, chans), BF16)]
        + [pltpu.SemaphoreType.REGULAR((2,))]
        + [dma((n,)) for n in (
            6, 16, 16, 2, zn, zn, zn, zn, 2,
            2, 2, 3, 3, 2,
            K, nq, nq, zn, zn, 3, 3, nq, nq, XS, XS, 2 + 2 * XS,
        )]
    )
    field = jax.ShapeDtypeStruct(signal.shape, BF16)
    conv, sgrad, wgrad = pl.pallas_call(
        kernel,
        out_shape=(field, field, jax.ShapeDtypeStruct((2, nq, piece, chans), BF16)),
        in_specs=[pl.BlockSpec(memory_space=pl.ANY)] * 6,
        out_specs=[pl.BlockSpec(memory_space=pl.ANY)] * 3,
        scratch_shapes=scratch,
        compiler_params=pltpu.CompilerParams(
            collective_id=0, has_side_effects=True, vmem_limit_bytes=60 * 2**20
        ),
        cost_estimate=pl.CostEstimate(flops=10**9, bytes_accessed=4 * 10**6, transcendentals=0),
    )(signal, cotangent, weights, band, cycle, support_width)
    return finish(conv, sgrad, wgrad.reshape(K, chans, chans))


def solution(mesh):
    placed = (P("lat", "lon", None), P("lat", "lon", None), P(), P(), P(), P())
    return jax.shard_map(
        local,
        mesh=mesh,
        in_specs=placed,
        out_specs=(P("lat", "lon", None), P("lat", "lon", None), P()),
        check_vma=False,
    )
```
